32 devices in a mesh: expert: 8 (over y, x, core), dp: 4 (over z).
Axes of the slice: x: 2, y: 2, z: 4, core: 2. Of those that a mesh axis runs over, the one named last changes fastest.
Arguments:
- tokens: bfloat16 [1024, 4096], P('expert'), may hold values from -6 to 6
- cotangent: bfloat16 [1024, 4096], P('expert'), may hold values from -3 to 3
- gate_weight: bfloat16 [8, 768, 4096], P('expert', 'dp'), may hold values from -0.09375 to 0.09375
- up_weight: bfloat16 [8, 768, 4096], P('expert', 'dp'), may hold values from -0.09375 to 0.09375
- down_weight: bfloat16 [8, 768, 4096], P('expert', 'dp'), may hold values from -0.21875 to 0.21875
- expert_ids: int32 [1024, 4], P('expert'), may hold values from 0 to 7, all different within a row; in each aligned block of 128 rows (0 to 127, 128 to 255, ...) at most 80 rows name the same one
- gates: bfloat16 [1024, 4], P('expert'), may hold values from 0.049804688 to 0.59765625
- swap_flags: int32 [4], replicated, may hold values 0 or 1
Outputs:
- input_grad: bfloat16 [1024, 4096], P('expert', 'dp')
- gate_grad: bfloat16 [1024, 4], P('expert')
- gate_weight_grad: bfloat16 [8, 768, 4096], P('expert', 'dp')
- up_weight_grad: bfloat16 [8, 768, 4096], P('expert', 'dp')
- down_weight_grad: bfloat16 [8, 768, 4096], P('expert', 'dp')
The draws below stay inside these ranges and needn't reach their ends.
Inputs may be any that keep to these rules, and one draw needn't show every extreme that they name: `expert_ids`: each row names 4 different experts. Among the rows of one device no expert is named more than 80 times, and in every draw some expert is named exactly 80 times by the rows of some device.
All inputs are finite; a program needn't handle non-finite values.
Results may differ from the reference program's by a relative error of at most 0.011.
Values may be sent and summed in bfloat16 or wider, within the bound.
No kernel may reach another device: no remote copies, remote signals or barrier semaphores. Data moves between devices by JAX's collectives and lax.ppermute only.
A program may use at most 128 MiB of HBM per device.

```python
import math
import jax
import jax.numpy as jnp
import numpy as np
from jax import lax

D = 4096
FF = 768
TOP = 4
TOK_DEV = 128
EXPERTS = 8
TOKENS = 1024
CAPACITY = 80
N_EXPERT = 8


def place_ends(values, own_key, smallest, high):
    place = [jax.random.randint(jax.random.fold_in(own_key, axis), (), 0, length) for axis, length in enumerate(values.shape)]
    longest = values.shape.index(max(values.shape))
    beside = place[:longest] + [(place[longest] + 1) % values.shape[longest]] + place[longest + 1:]
    return values.at[tuple(place)].set(smallest).at[tuple(beside)].set(high)


def block_levels(key, extent, pieces, least, top_value):
    def one(dim, shards_of):
        steps = jax.random.uniform(jax.random.fold_in(jax.random.fold_in(key, 6), dim), (shards_of,), jnp.float32, least / len(pieces), top_value / len(pieces))
        return jnp.repeat(jnp.exp(steps), extent[dim] // shards_of).reshape((-1,) + (1,) * (len(extent) - dim - 1))

    factor_of = one(*pieces[0])
    for cut in pieces[1:]:
        factor_of = factor_of * one(*cut)
    return factor_of


def shared_out(stream_key, own, number, rows, amount, top, bound, lean):
    sequence = jax.random.permutation(stream_key, amount)
    crowded, ordinary = load_shares(amount, rows * top, bound, lean, True), load_shares(amount, rows * top, bound, lean, False)
    places = jnp.arange(amount)

    def named(tallies, rotation):
        used = int((tallies > 0).sum())
        fixed = max(1, used // 4)
        moved = fixed + (places - fixed + rotation * (used - fixed)) % max(1, amount - fixed)
        return jnp.zeros((amount,), jnp.int32).at[sequence[jnp.where(places < fixed, places, moved)]].set(jnp.asarray(tallies, jnp.int32))

    tallies = jnp.where(number % 4 == 0, named(crowded, number // 4), named(ordinary, number - number // 4 - 1))
    mixed = jax.random.permutation(jax.random.fold_in(own, 3), amount)
    giver, taker = mixed[0:amount // 2 * 2:2], mixed[1:amount // 2 * 2:2]
    margin = jnp.minimum(tallies[giver] - 1, bound - tallies[taker]) // 2
    margin = jnp.where((giver == sequence[0]) | (taker == sequence[0]) | (tallies[taker] == 0), 0, jnp.maximum(margin, 0))
    moved = jax.random.randint(jax.random.fold_in(own, 4), (amount // 2,), 0, 1 << 20) % (margin + 1)
    tallies = tallies.at[giver].add(-moved).at[taker].add(moved)
    items = jnp.searchsorted(jnp.cumsum(tallies), jnp.arange(rows * top), side="right").astype(jnp.int32)
    table = items.reshape(top, rows).T
    table = table[jax.random.permutation(jax.random.fold_in(own, 1), rows)]
    rotation = jax.random.randint(jax.random.fold_in(own, 2), (rows, 1), 0, top)
    return jnp.take_along_axis(table, (jnp.arange(top)[None, :] + rotation) % top, axis=1)


def load_shares(amount, total, most, skew, full):
    portions = [(1 << 20) // math.isqrt(grade ** skew) + 1 for grade in range(1, amount + 1)]
    largest = most if full else min(most, max(-(-total // amount), total * portions[0] // sum(portions)))
    least = 1 if total - largest >= amount - 1 else 0
    given, rest = [largest] + [least] * (amount - 1), total - largest - least * (amount - 1)
    while rest > 0:
        free = [i for i in range(1, amount) if given[i] < largest] or [i for i in range(1, amount) if given[i] < most]
        pool, budget = sum([portions[i] for i in free]), rest
        for i in free:
            extra = min(most - given[i], max(1, budget * portions[i] // pool), rest)
            given[i] = given[i] + extra
            rest = rest - extra
    return np.array(given)


def normal_values(rng, extent, width, most, shards=(), kind=jnp.bfloat16):
    gain = block_levels(rng, extent, shards, -0.22, 0.18) if shards else 1.0
    result = jax.random.normal(rng, extent, jnp.float32) * width * gain
    return jnp.minimum(jnp.maximum(result, -most), most).astype(kind)


def setup_inputs(seed: int = 0) -> dict:
    splits = jax.random.split(jax.random.key(seed), 9)
    tokens = normal_values(splits[0], (TOKENS, D), 1.0, 6.0, ((0, 8),))
    cotangent = normal_values(splits[1], (TOKENS, D), 0.5, 3.0, ((0, 8),))
    gate_weight = normal_values(splits[2], (EXPERTS, FF, D), D ** -0.5, 0.09375, ((0, 8), (1, 4)))
    up_weight = normal_values(splits[3], (EXPERTS, FF, D), D ** -0.5, 0.09375, ((0, 8), (1, 4)))
    down_weight = normal_values(splits[4], (EXPERTS, FF, D), FF ** -0.5, 0.21875, ((0, 8), (1, 4)))
    expert_ids_keys = jax.random.split(jax.random.fold_in(splits[5], 1), TOKENS // TOK_DEV)
    expert_ids_turns = jax.random.permutation(jax.random.fold_in(splits[5], 3), TOKENS // TOK_DEV)
    expert_ids = jax.vmap(lambda own, number: shared_out(jax.random.fold_in(splits[5], 2), own, number, TOK_DEV, EXPERTS, TOP, CAPACITY, 2))(expert_ids_keys, expert_ids_turns).reshape((TOKENS, TOP))
    gates = jnp.clip(jnp.exp(math.log(0.59765625) - 2.4849066 * jax.random.uniform(splits[6], (TOKENS, TOP), jnp.float32) ** block_levels(splits[6], (TOKENS, TOP), ((0, 8),), -0.2, 0.2)), 0.049804688, 0.59765625).astype(jnp.bfloat16)
    swap_flags = place_ends((jax.random.randint(splits[7], (EXPERTS // 2,), 0, 2) < 1).astype(jnp.int32), jax.random.fold_in(splits[7], 1), 0, 1)
    return dict(tokens=tokens, cotangent=cotangent, gate_weight=gate_weight, up_weight=up_weight, down_weight=down_weight, expert_ids=expert_ids, gates=gates, swap_flags=swap_flags)


def expert_pass(x_rows, dy_rows, gate_rows, w_gate, w_up, w_down):
    pre_gate = lax.dot_general(x_rows, w_gate, (((1,), (1,)), ((), ())), preferred_element_type=jnp.float32)
    pre_up = lax.dot_general(x_rows, w_up, (((1,), (1,)), ((), ())), preferred_element_type=jnp.float32)
    sigma = jax.nn.sigmoid(pre_gate)
    active = pre_gate * sigma
    hidden = (active * pre_up).astype(jnp.bfloat16)
    back = lax.dot_general(dy_rows, w_down, (((1,), (1,)), ((), ())), preferred_element_type=jnp.float32)
    score = jnp.sum(hidden.astype(jnp.float32) * back, axis=1)
    grad_hidden = gate_rows.astype(jnp.float32)[:, None] * back
    slope = sigma * (1.0 + pre_gate * (1.0 - sigma))
    grad_gate = (grad_hidden * pre_up * slope).astype(jnp.bfloat16)
    grad_up = (grad_hidden * active).astype(jnp.bfloat16)
    input_rows = jnp.dot(grad_gate, w_gate, preferred_element_type=jnp.float32)
    input_rows = input_rows + jnp.dot(grad_up, w_up, preferred_element_type=jnp.float32)
    scaled = gate_rows[:, None] * dy_rows
    grad_wgate = lax.dot_general(grad_gate, x_rows, (((0,), (0,)), ((), ())), preferred_element_type=jnp.float32)
    grad_wup = lax.dot_general(grad_up, x_rows, (((0,), (0,)), ((), ())), preferred_element_type=jnp.float32)
    grad_wdown = lax.dot_general(hidden, scaled, (((0,), (0,)), ((), ())), preferred_element_type=jnp.float32)
    return (grad_wgate.astype(jnp.bfloat16), grad_wup.astype(jnp.bfloat16), grad_wdown.astype(jnp.bfloat16),
            input_rows.astype(jnp.bfloat16), score)


def reference(tokens, cotangent, gate_weight, up_weight, down_weight, expert_ids, gates, swap_flags):
    copies = TOKENS * TOP
    flat_ids = expert_ids.reshape(-1).astype(jnp.int32)
    flat_gates = gates.reshape(-1)
    sender = (jnp.arange(copies) // (TOK_DEV * TOP)).astype(jnp.int32)
    blocked = flat_ids.reshape(N_EXPERT, TOK_DEV * TOP)
    onehot = (blocked[:, :, None] == jnp.arange(EXPERTS, dtype=jnp.int32)[None, None, :]).astype(jnp.int32)
    earlier = jnp.cumsum(onehot, axis=1) - onehot
    position = jnp.sum(earlier * onehot, axis=2).reshape(-1).astype(jnp.int32)
    row_index = (sender * CAPACITY + position).astype(jnp.int32)
    table = jnp.zeros((EXPERTS, N_EXPERT * CAPACITY), jnp.int32)
    table = table.at[flat_ids, row_index].set(jnp.arange(copies, dtype=jnp.int32) + 1)

    def per_expert(packed):
        w_gate, w_up, w_down, source = packed
        filled = source > 0
        copy_index = jnp.maximum(source - 1, 0).astype(jnp.int32)
        token_index = (copy_index // TOP).astype(jnp.int32)
        x_rows = jnp.where(filled[:, None], tokens[token_index], 0)
        dy_rows = jnp.where(filled[:, None], cotangent[token_index], 0)
        gate_rows = jnp.where(filled, flat_gates[copy_index], 0)
        return expert_pass(x_rows, dy_rows, gate_rows, w_gate, w_up, w_down)

    grad_wgate, grad_wup, grad_wdown, input_rows, scores = lax.map(
        per_expert, (gate_weight, up_weight, down_weight, table))
    per_copy = input_rows[flat_ids, row_index].reshape(TOKENS, TOP, D)
    input_grad = jnp.sum(per_copy.astype(jnp.float32), axis=1).astype(jnp.bfloat16)
    gate_grad = scores[flat_ids, row_index].astype(jnp.bfloat16).reshape(TOKENS, TOP)
    half_axis = EXPERTS // 2
    slots = jnp.arange(EXPERTS, dtype=jnp.int32)
    pair_flag = swap_flags[slots % half_axis]
    holder = jnp.where(pair_flag == 1, (slots + half_axis) % EXPERTS, slots).astype(jnp.int32)
    return input_grad, gate_grad, grad_wgate[holder], grad_wup[holder], grad_wdown[holder]
```

```python
import jax
import jax.numpy as jnp
from jax import lax
from jax.sharding import PartitionSpec as P


def from_behind(value, axis, by):
    devices = lax.axis_size(axis)
    return lax.ppermute(value, axis, [(i, (i + by) % devices) for i in range(devices)])


def pair_lookup(experts, pair_flags, half_axis):
    match = experts[:, None] % half_axis == jnp.arange(half_axis, dtype=jnp.int32)[None, :]
    return jnp.sum(jnp.where(match, pair_flags[None, :], 0), axis=1)


CONTRACT_LAST = (((1,), (1,)), ((), ()))
CONTRACT_ROWS = (((0,), (0,)), ((), ()))


def whole_shards(tokens, cotangent, gate_weight, up_weight, down_weight, expert_ids, gates, swap_flags):
    expert_count = lax.axis_size("expert")
    half_axis = expert_count // 2
    me = lax.axis_index("expert")
    row_count, model_width = tokens.shape
    f32, bf16 = jnp.float32, jnp.bfloat16
    own_flag = pair_lookup(jnp.reshape(me, (1,)), swap_flags, half_axis)[0]

    named = expert_ids[:, :, None] == jnp.arange(expert_count, dtype=jnp.int32)[None, None, :]
    table = jnp.sum(jnp.where(named, gates[:, :, None].astype(f32), 0), axis=1)
    all_gates = lax.all_gather(table, "expert", tiled=True)
    x = lax.all_gather(tokens, "expert", tiled=True)
    dy = lax.all_gather(cotangent, "expert", tiled=True)
    mine = jnp.arange(expert_count, dtype=jnp.int32)[None, :] == me
    g = jnp.sum(jnp.where(mine, all_gates, 0), axis=1)[:, None]

    w_gate, w_up, w_down = gate_weight[0], up_weight[0], down_weight[0]
    pre_gate = lax.dot_general(x, w_gate, CONTRACT_LAST, preferred_element_type=f32)
    pre_up = lax.dot_general(x, w_up, CONTRACT_LAST, preferred_element_type=f32)
    back = lax.dot_general(dy, w_down, CONTRACT_LAST, preferred_element_type=f32)
    sigma = jax.nn.sigmoid(pre_gate)
    active = pre_gate * sigma
    hidden = active * pre_up
    score_part = jnp.sum(hidden * back, axis=1)
    grad_hidden = g * back
    slope = sigma * (1.0 + pre_gate * (1.0 - sigma))
    grad_gate = (grad_hidden * pre_up * slope).astype(bf16)
    grad_up = (grad_hidden * active).astype(bf16)
    weighted = (g * hidden).astype(bf16)

    acts = jnp.concatenate([grad_gate, grad_up, weighted], axis=1)
    arrived = from_behind(acts, "expert", half_axis)
    acts = jnp.where(own_flag == 1, arrived, acts)
    width = grad_gate.shape[1]

    part = jnp.dot(grad_gate, w_gate, preferred_element_type=f32)
    part = part + jnp.dot(grad_up, w_up, preferred_element_type=f32)
    share = lax.psum_scatter(part.astype(bf16), "expert", scatter_dimension=0, tiled=True)
    input_grad = lax.psum_scatter(share, "dp", scatter_dimension=1, tiled=True)

    scores = lax.psum(score_part, "dp")
    scores = lax.all_to_all(
        scores.astype(bf16).reshape(expert_count, row_count), "expert", split_axis=0, concat_axis=0, tiled=True
    )
    picked = jnp.where(named, scores.T[:, None, :].astype(f32), 0)
    gate_grad = jnp.sum(picked, axis=2).astype(bf16)

    grad_wboth = lax.dot_general(acts[:, : 2 * width], x, CONTRACT_ROWS, preferred_element_type=f32)
    grad_wdown = lax.dot_general(acts[:, 2 * width :], dy, CONTRACT_ROWS, preferred_element_type=f32)
    grad_wboth = grad_wboth.astype(bf16)
    return (
        input_grad.astype(bf16),
        gate_grad,
        grad_wboth[None, :width],
        grad_wboth[None, width:],
        grad_wdown.astype(bf16)[None],
    )


def packed_shards(tokens, cotangent, gate_weight, up_weight, down_weight, expert_ids, gates, swap_flags):
    expert_count = lax.axis_size("expert")
    half_axis = expert_count // 2
    my_slot = lax.axis_index("expert")
    row_count, model_width = tokens.shape
    routed = expert_ids.shape[1]
    capacity = row_count * routed * 5 // (4 * expert_count)
    groups = lax.axis_size("dp")
    quarter = model_width // groups
    own_flag = pair_lookup(jnp.reshape(my_slot, (1,)), swap_flags, half_axis)[0]
    flat_ids = expert_ids.reshape(-1)
    weights = (gate_weight, up_weight, down_weight)
    arrived = from_behind((gate_weight, up_weight, down_weight), "expert", half_axis)
    weights = tuple(
        (jnp.where(own_flag == 1, fresh, stay) for fresh, stay in zip(arrived, weights))
    )
    flipped = pair_lookup(flat_ids, swap_flags, half_axis)
    target = jnp.where(flipped == 1, (flat_ids + half_axis) % expert_count, flat_ids)
    copies = row_count * routed
    onehot = (target[:, None] == jnp.arange(expert_count, dtype=jnp.int32)[None, :]).astype(
        jnp.int32
    )
    earlier = jnp.cumsum(onehot, axis=0) - onehot
    position = jnp.sum(earlier * onehot, axis=1)
    buffer_index = target * capacity + position
    source = jnp.zeros((expert_count * capacity,), jnp.int32)
    source = source.at[buffer_index].set(jnp.arange(copies, dtype=jnp.int32) + 1)
    filled = source > 0
    copy_index = jnp.maximum(source - 1, 0)
    token_index = copy_index // routed
    x_buffer = jnp.where(filled[:, None], tokens[token_index], 0)
    dy_buffer = jnp.where(filled[:, None], cotangent[token_index], 0)
    gate_buffer = jnp.where(filled, gates.reshape(-1)[copy_index], 0)
    x_rows, dy_rows, gate_rows = (
        lax.all_to_all(x_buffer, "expert", split_axis=0, concat_axis=0, tiled=True),
        lax.all_to_all(dy_buffer, "expert", split_axis=0, concat_axis=0, tiled=True),
        lax.all_to_all(gate_buffer, "expert", split_axis=0, concat_axis=0, tiled=True),
    )
    w_gate = weights[0][0]
    w_up = weights[1][0]
    w_down = weights[2][0]
    contract_last = (((1,), (1,)), ((), ()))
    pre_gate = lax.dot_general(x_rows, w_gate, contract_last, preferred_element_type=jnp.float32)
    pre_up = lax.dot_general(x_rows, w_up, contract_last, preferred_element_type=jnp.float32)
    sigma = jax.nn.sigmoid(pre_gate)
    active = pre_gate * sigma
    hidden = (active * pre_up).astype(jnp.bfloat16)
    back = lax.dot_general(dy_rows, w_down, contract_last, preferred_element_type=jnp.float32)
    score_part = jnp.sum(hidden.astype(jnp.float32) * back, axis=1)
    grad_hidden = gate_rows.astype(jnp.float32)[:, None] * back
    slope = sigma * (1.0 + pre_gate * (1.0 - sigma))
    grad_gate = (grad_hidden * pre_up * slope).astype(jnp.bfloat16)
    grad_up = (grad_hidden * active).astype(jnp.bfloat16)
    input_part = jnp.dot(grad_gate, w_gate, preferred_element_type=jnp.float32)
    input_part = input_part + jnp.dot(grad_up, w_up, preferred_element_type=jnp.float32)
    scaled = gate_rows[:, None] * dy_rows
    contract_rows = (((0,), (0,)), ((), ()))
    grad_wgate = lax.dot_general(
        grad_gate, x_rows, contract_rows, preferred_element_type=jnp.float32
    )
    grad_wup = lax.dot_general(grad_up, x_rows, contract_rows, preferred_element_type=jnp.float32)
    grad_wdown = lax.dot_general(hidden, scaled, contract_rows, preferred_element_type=jnp.float32)
    scores = lax.psum(score_part, "dp")
    input_share = lax.psum_scatter(input_part, "dp", scatter_dimension=1, tiled=True).astype(
        jnp.bfloat16
    )
    back_rows, back_scores = (
        lax.all_to_all(input_share, "expert", split_axis=0, concat_axis=0, tiled=True),
        lax.all_to_all(
            scores.astype(jnp.bfloat16), "expert", split_axis=0, concat_axis=0, tiled=True
        ),
    )
    per_copy = back_rows[buffer_index].reshape(row_count, routed, quarter)
    input_grad = jnp.sum(per_copy.astype(jnp.float32), axis=1).astype(jnp.bfloat16)
    gate_grad = back_scores[buffer_index].reshape(row_count, routed)
    gradients = (
        grad_wgate.astype(jnp.bfloat16)[None],
        grad_wup.astype(jnp.bfloat16)[None],
        grad_wdown.astype(jnp.bfloat16)[None],
    )
    return (input_grad, gate_grad, gradients[0], gradients[1], gradients[2])


def chosen(tokens, cotangent, gate_weight, up_weight, down_weight, expert_ids, gates, swap_flags):
    capacity = tokens.shape[0] * expert_ids.shape[1] * 5 // (4 * lax.axis_size("expert"))
    body = whole_shards if 2 * capacity >= tokens.shape[0] else packed_shards
    return body(tokens, cotangent, gate_weight, up_weight, down_weight, expert_ids, gates, swap_flags)


def solution(mesh):
    placed = (
        P("expert", None),
        P("expert", None),
        P("expert", "dp", None),
        P("expert", "dp", None),
        P("expert", "dp", None),
        P("expert", None),
        P("expert", None),
        P(),
    )
    return jax.shard_map(
        chosen,
        mesh=mesh,
        in_specs=placed,
        out_specs=(
            P("expert", "dp"),
            P("expert", None),
            P("expert", "dp", None),
            P("expert", "dp", None),
            P("expert", "dp", None),
        ),
        check_vma=False,
    )
```

```python
import functools

import jax
import jax.numpy as jnp
from jax import lax
from jax.experimental import pallas as pl
from jax.experimental.pallas import tpu as pltpu
from jax.sharding import PartitionSpec as P


CONTRACT_LAST = (((1,), (1,)), ((), ()))
CONTRACT_ROWS = (((0,), (0,)), ((), ()))
VMEM = 56 * 1024 * 1024


def from_behind(value, axis, by):
    devices = lax.axis_size(axis)
    return lax.ppermute(value, axis, [(i, (i + by) % devices) for i in range(devices)])


def swap(value, axis, by):
    return lax.ppermute(value, axis, [(i, i ^ by) for i in range(lax.axis_size(axis))])


def pair_lookup(experts, pair_flags, half_axis):
    match = experts[:, None] % half_axis == jnp.arange(half_axis, dtype=jnp.int32)[None, :]
    return jnp.sum(jnp.where(match, pair_flags[None, :], 0), axis=1)


def activations_kernel(blocks, parts, where_ref, gates_ref, *refs):
    count = len(blocks)
    x_refs, dy_refs = refs[:count], refs[count : 2 * count]
    gate_ref, up_ref, down_ref = refs[2 * count : 2 * count + 3]
    acts_ref, score_ref, keep_ref, give_ref = refs[2 * count + 3 : 2 * count + 7]
    x_all, dy_all, in_all, down_all, sems = refs[2 * count + 7 :]
    rows, width = x_refs[0].shape
    units = gate_ref.shape[0]
    chunk = width // parts
    copies = []
    for part in range(parts):
        columns = pl.ds(part * chunk, chunk)
        moves = [(gate_ref, in_all, 0, units), (up_ref, in_all, units, units), (down_ref, down_all, 0, units)]
        moves += [(ref, x_all, i * rows, rows) for i, ref in enumerate(x_refs)]
        moves += [(ref, dy_all, i * rows, rows) for i, ref in enumerate(dy_refs)]
        copies.append(
            [
                pltpu.make_async_copy(
                    ref.at[:, columns], target.at[pl.ds(start, size), columns], sems.at[part, i]
                )
                for i, (ref, target, start, size) in enumerate(moves)
            ]
        )
        for copy in copies[-1]:
            copy.start()
    me, group = where_ref[0], where_ref[1]
    pre, back = None, None
    for part in range(parts):
        for copy in copies[part]:
            copy.wait()
        columns = pl.ds(part * chunk, chunk)
        one = lax.dot_general(
            in_all[:, columns], x_all[:, columns], CONTRACT_LAST, preferred_element_type=jnp.float32
        )
        two = lax.dot_general(
            down_all[:, columns], dy_all[:, columns], CONTRACT_LAST, preferred_element_type=jnp.float32
        )
        pre = one if pre is None else pre + one
        back = two if back is None else back + two
    pre_gate, pre_up = pre[:units], pre[units:]
    g = jnp.concatenate([gates_ref[pl.ds(me ^ block, 1), :] for block in blocks], axis=1)
    sigma = jax.nn.sigmoid(pre_gate)
    active = pre_gate * sigma
    hidden = active * pre_up
    score_ref[...] = jnp.sum(hidden * back, axis=0, keepdims=True)
    grad_hidden = g * back
    slope = sigma * (1.0 + pre_gate * (1.0 - sigma))
    acts_ref[pl.ds(0, units), :] = (grad_hidden * pre_up * slope).astype(jnp.bfloat16)
    acts_ref[pl.ds(units, units), :] = (grad_hidden * active).astype(jnp.bfloat16)
    acts_ref[pl.ds(2 * units, units), :] = (g * hidden).astype(jnp.bfloat16)
    both = acts_ref[pl.ds(0, 2 * units), :]
    for part in range(parts):
        columns = pl.ds(pl.multiple_of((group ^ part) * chunk, chunk), chunk)
        share = lax.dot_general(both, in_all[:, columns], CONTRACT_ROWS, preferred_element_type=jnp.float32)
        share = share.astype(jnp.bfloat16)
        for pair in range(count // 2):
            keep_ref[part, pl.ds(pair * rows, rows), :] = share[2 * pair * rows : (2 * pair + 1) * rows]
            give_ref[part, pl.ds(pair * rows, rows), :] = share[(2 * pair + 1) * rows : (2 * pair + 2) * rows]


def activations(blocks, parts, where, gates, x_blocks, dy_blocks, w_gate, w_up, w_down):
    count = len(blocks)
    rows, width = x_blocks[0].shape
    units = w_gate.shape[0]
    bf16 = jnp.bfloat16
    share = jax.ShapeDtypeStruct((parts, count // 2 * rows, width // parts), bf16)
    return pl.pallas_call(
        functools.partial(activations_kernel, blocks, parts),
        out_shape=(
            jax.ShapeDtypeStruct((3 * units, count * rows), bf16),
            jax.ShapeDtypeStruct((1, count * rows), jnp.float32),
            share,
            share,
        ),
        in_specs=[pl.BlockSpec(memory_space=pltpu.SMEM), pl.BlockSpec(memory_space=pltpu.VMEM)]
        + [pl.BlockSpec(memory_space=pl.ANY)] * (2 * count + 3),
        out_specs=[pl.BlockSpec(memory_space=pltpu.VMEM)] * 4,
        scratch_shapes=[
            pltpu.VMEM((count * rows, width), bf16),
            pltpu.VMEM((count * rows, width), bf16),
            pltpu.VMEM((2 * units, width), bf16),
            pltpu.VMEM((units, width), bf16),
            pltpu.SemaphoreType.DMA((parts, 2 * count + 3)),
        ],
        compiler_params=pltpu.CompilerParams(vmem_limit_bytes=VMEM),
        name="activations",
    )(where, gates, *x_blocks, *dy_blocks, w_gate, w_up, w_down)


def weight_grads_kernel(order, parts, flag_ref, *refs):
    count = len(order)
    x_refs, dy_refs = refs[:count], refs[count : 2 * count]
    own_ref, other_ref = refs[2 * count : 2 * count + 2]
    outs = refs[2 * count + 2 : 2 * count + 5]
    x_all, dy_all, acts, sems = refs[2 * count + 5 :]
    rows, width = x_refs[0].shape
    units = outs[0].shape[1]
    chunk = width // parts
    copies = []
    for part in range(parts):
        columns = pl.ds(part * chunk, chunk)
        moves = [(ref, x_all, i * rows) for i, ref in enumerate(x_refs)]
        moves += [(ref, dy_all, i * rows) for i, ref in enumerate(dy_refs)]
        copies.append(
            [
                pltpu.make_async_copy(ref.at[:, columns], target.at[pl.ds(start, rows), columns], sems.at[part, i])
                for i, (ref, target, start) in enumerate(moves)
            ]
        )
        for copy in copies[-1]:
            copy.start()
    half = count // 2
    for place, block in enumerate(order):
        theirs = order.index(block ^ half)
        arrived = other_ref[:, pl.ds(theirs * rows, rows)]
        stay = own_ref[:, pl.ds(place * rows, rows)]
        acts[:, pl.ds(place * rows, rows)] = jnp.where(flag_ref[0] == 1, arrived, stay)
    for part in range(parts):
        for copy in copies[part]:
            copy.wait()
        columns = pl.ds(part * chunk, chunk)
        both = jnp.dot(acts[pl.ds(0, 2 * units), :], x_all[:, columns], preferred_element_type=jnp.float32)
        down = jnp.dot(acts[pl.ds(2 * units, units), :], dy_all[:, columns], preferred_element_type=jnp.float32)
        outs[0][0, :, columns] = both[:units].astype(jnp.bfloat16)
        outs[1][0, :, columns] = both[units:].astype(jnp.bfloat16)
        outs[2][0, :, columns] = down.astype(jnp.bfloat16)


def weight_grads(order, flag, x_blocks, dy_blocks, own, other):
    count, parts = len(order), 8
    rows, width = x_blocks[0].shape
    units = own.shape[0] // 3
    bf16 = jnp.bfloat16
    return pl.pallas_call(
        functools.partial(weight_grads_kernel, order, parts),
        out_shape=(jax.ShapeDtypeStruct((1, units, width), bf16),) * 3,
        in_specs=[pl.BlockSpec(memory_space=pltpu.SMEM)]
        + [pl.BlockSpec(memory_space=pl.ANY)] * (2 * count)
        + [pl.BlockSpec(memory_space=pltpu.VMEM)] * 2,
        out_specs=[pl.BlockSpec(memory_space=pltpu.VMEM)] * 3,
        scratch_shapes=[
            pltpu.VMEM((count * rows, width), bf16),
            pltpu.VMEM((count * rows, width), bf16),
            pltpu.VMEM((3 * units, count * rows), bf16),
            pltpu.SemaphoreType.DMA((parts, 2 * count)),
        ],
        compiler_params=pltpu.CompilerParams(vmem_limit_bytes=VMEM),
        name="weight_grads",
    )(flag, *x_blocks, *dy_blocks, own, other)


CORE, ACROSS_X, ACROSS_Y = 1, 2, 4


def whole_shards(tokens, cotangent, gate_weight, up_weight, down_weight, expert_ids, gates, swap_flags):
    expert_count = lax.axis_size("expert")
    half_axis = expert_count // 2
    me, group = lax.axis_index("expert"), lax.axis_index("dp")
    row_count = tokens.shape[0]
    parts = lax.axis_size("dp")
    f32, bf16 = jnp.float32, jnp.bfloat16
    own_flag = pair_lookup(jnp.reshape(me, (1,)), swap_flags, half_axis)
    where = jnp.stack([me, group]).astype(jnp.int32)

    x, dy = {0: tokens}, {0: cotangent}
    x[2], dy[4] = swap(tokens, "expert", ACROSS_X), swap(cotangent, "expert", ACROSS_Y)
    x[1], dy[1] = swap(tokens, "expert", CORE), swap(cotangent, "expert", CORE)
    x[4], dy[2] = swap(tokens, "expert", ACROSS_Y), swap(cotangent, "expert", ACROSS_X)
    x[6], dy[6] = swap(x[2], "expert", ACROSS_Y), swap(dy[4], "expert", ACROSS_X)
    for block in (2, 4, 6):
        x[block + 1], dy[block + 1] = swap(x[block], "expert", CORE), swap(dy[block], "expert", CORE)

    named = expert_ids[:, :, None] == jnp.arange(expert_count, dtype=jnp.int32)[None, None, :]
    table = jnp.sum(jnp.where(named, gates[:, :, None].astype(f32), 0), axis=1)
    gate_rows = lax.all_to_all(table.T, "expert", split_axis=0, concat_axis=0, tiled=True)

    weights = (gate_weight[0], up_weight[0], down_weight[0])
    groups = ((0, 1), (2, 3, 4, 5), (6, 7))
    order = sum(groups, ())
    acts, scores, totals = [], [], {}
    for blocks in groups:
        act, score, keep, give = activations(
            blocks, parts, where, gate_rows, [x[b] for b in blocks], [dy[b] for b in blocks], *weights
        )
        acts.append(act)
        scores.append(score)
        both = keep + swap(give, "expert", CORE)
        total = both[0].astype(f32)
        for part in range(1, parts):
            total = total + swap(both[part], "dp", part).astype(f32)
        for pair in range(len(blocks) // 2):
            totals[blocks[2 * pair]] = total[pair * row_count : (pair + 1) * row_count]
    input_grad = totals[0]
    for block in (ACROSS_X, ACROSS_Y, ACROSS_X | ACROSS_Y):
        input_grad = input_grad + swap(totals[block].astype(bf16), "expert", block).astype(f32)

    acts = jnp.concatenate(acts, axis=1)
    grads = weight_grads(order, own_flag, [x[b] for b in order], [dy[b] for b in order], acts, swap(acts, "expert", half_axis))

    score_rows = lax.psum(jnp.concatenate(scores, axis=1).reshape(expert_count, row_count), "dp").astype(bf16)
    score_rows = jnp.take(score_rows, jnp.arange(expert_count, dtype=jnp.int32) ^ me, axis=0)
    score_rows = lax.all_to_all(score_rows, "expert", split_axis=0, concat_axis=0, tiled=True)
    gate_grad = jnp.sum(jnp.where(named, score_rows.T[:, None, :].astype(f32), 0), axis=2)
    return (input_grad.astype(bf16), gate_grad.astype(bf16), *grads)


def packed_shards(tokens, cotangent, gate_weight, up_weight, down_weight, expert_ids, gates, swap_flags):
    expert_count = lax.axis_size("expert")
    half_axis = expert_count // 2
    my_slot = lax.axis_index("expert")
    row_count, model_width = tokens.shape
    routed = expert_ids.shape[1]
    capacity = row_count * routed * 5 // (4 * expert_count)
    groups = lax.axis_size("dp")
    quarter = model_width // groups
    own_flag = pair_lookup(jnp.reshape(my_slot, (1,)), swap_flags, half_axis)[0]
    flat_ids = expert_ids.reshape(-1)
    weights = (gate_weight, up_weight, down_weight)
    arrived = from_behind((gate_weight, up_weight, down_weight), "expert", half_axis)
    weights = tuple(
        (jnp.where(own_flag == 1, fresh, stay) for fresh, stay in zip(arrived, weights))
    )
    flipped = pair_lookup(flat_ids, swap_flags, half_axis)
    target = jnp.where(flipped == 1, (flat_ids + half_axis) % expert_count, flat_ids)
    copies = row_count * routed
    onehot = (target[:, None] == jnp.arange(expert_count, dtype=jnp.int32)[None, :]).astype(
        jnp.int32
    )
    earlier = jnp.cumsum(onehot, axis=0) - onehot
    position = jnp.sum(earlier * onehot, axis=1)
    buffer_index = target * capacity + position
    source = jnp.zeros((expert_count * capacity,), jnp.int32)
    source = source.at[buffer_index].set(jnp.arange(copies, dtype=jnp.int32) + 1)
    filled = source > 0
    copy_index = jnp.maximum(source - 1, 0)
    token_index = copy_index // routed
    x_buffer = jnp.where(filled[:, None], tokens[token_index], 0)
    dy_buffer = jnp.where(filled[:, None], cotangent[token_index], 0)
    gate_buffer = jnp.where(filled, gates.reshape(-1)[copy_index], 0)
    x_rows, dy_rows, gate_rows = (
        lax.all_to_all(x_buffer, "expert", split_axis=0, concat_axis=0, tiled=True),
        lax.all_to_all(dy_buffer, "expert", split_axis=0, concat_axis=0, tiled=True),
        lax.all_to_all(gate_buffer, "expert", split_axis=0, concat_axis=0, tiled=True),
    )
    w_gate = weights[0][0]
    w_up = weights[1][0]
    w_down = weights[2][0]
    contract_last = (((1,), (1,)), ((), ()))
    pre_gate = lax.dot_general(x_rows, w_gate, contract_last, preferred_element_type=jnp.float32)
    pre_up = lax.dot_general(x_rows, w_up, contract_last, preferred_element_type=jnp.float32)
    sigma = jax.nn.sigmoid(pre_gate)
    active = pre_gate * sigma
    hidden = (active * pre_up).astype(jnp.bfloat16)
    back = lax.dot_general(dy_rows, w_down, contract_last, preferred_element_type=jnp.float32)
    score_part = jnp.sum(hidden.astype(jnp.float32) * back, axis=1)
    grad_hidden = gate_rows.astype(jnp.float32)[:, None] * back
    slope = sigma * (1.0 + pre_gate * (1.0 - sigma))
    grad_gate = (grad_hidden * pre_up * slope).astype(jnp.bfloat16)
    grad_up = (grad_hidden * active).astype(jnp.bfloat16)
    input_part = jnp.dot(grad_gate, w_gate, preferred_element_type=jnp.float32)
    input_part = input_part + jnp.dot(grad_up, w_up, preferred_element_type=jnp.float32)
    scaled = gate_rows[:, None] * dy_rows
    contract_rows = (((0,), (0,)), ((), ()))
    grad_wgate = lax.dot_general(
        grad_gate, x_rows, contract_rows, preferred_element_type=jnp.float32
    )
    grad_wup = lax.dot_general(grad_up, x_rows, contract_rows, preferred_element_type=jnp.float32)
    grad_wdown = lax.dot_general(hidden, scaled, contract_rows, preferred_element_type=jnp.float32)
    scores = lax.psum(score_part, "dp")
    input_share = lax.psum_scatter(input_part, "dp", scatter_dimension=1, tiled=True).astype(
        jnp.bfloat16
    )
    back_rows, back_scores = (
        lax.all_to_all(input_share, "expert", split_axis=0, concat_axis=0, tiled=True),
        lax.all_to_all(
            scores.astype(jnp.bfloat16), "expert", split_axis=0, concat_axis=0, tiled=True
        ),
    )
    per_copy = back_rows[buffer_index].reshape(row_count, routed, quarter)
    input_grad = jnp.sum(per_copy.astype(jnp.float32), axis=1).astype(jnp.bfloat16)
    gate_grad = back_scores[buffer_index].reshape(row_count, routed)
    gradients = (
        grad_wgate.astype(jnp.bfloat16)[None],
        grad_wup.astype(jnp.bfloat16)[None],
        grad_wdown.astype(jnp.bfloat16)[None],
    )
    return (input_grad, gate_grad, gradients[0], gradients[1], gradients[2])


def chosen(tokens, cotangent, gate_weight, up_weight, down_weight, expert_ids, gates, swap_flags):
    capacity = tokens.shape[0] * expert_ids.shape[1] * 5 // (4 * lax.axis_size("expert"))
    body = whole_shards if 2 * capacity >= tokens.shape[0] else packed_shards
    return body(tokens, cotangent, gate_weight, up_weight, down_weight, expert_ids, gates, swap_flags)


def solution(mesh):
    placed = (
        P("expert", None),
        P("expert", None),
        P("expert", "dp", None),
        P("expert", "dp", None),
        P("expert", "dp", None),
        P("expert", None),
        P("expert", None),
        P(),
    )
    return jax.shard_map(
        chosen,
        mesh=mesh,
        in_specs=placed,
        out_specs=(
            P("expert", "dp"),
            P("expert", None),
            P("expert", "dp", None),
            P("expert", "dp", None),
            P("expert", "dp", None),
        ),
        check_vma=False,
    )
```

```python
import functools

import jax
import jax.numpy as jnp
from jax import lax
from jax.experimental import pallas as pl
from jax.experimental.pallas import tpu as pltpu
from jax.sharding import PartitionSpec as P


CONTRACT_LAST = (((1,), (1,)), ((), ()))
CONTRACT_ROWS = (((0,), (0,)), ((), ()))
VMEM = 56 * 1024 * 1024


def from_behind(value, axis, by):
    devices = lax.axis_size(axis)
    return lax.ppermute(value, axis, [(i, (i + by) % devices) for i in range(devices)])


def swap(value, axis, by):
    return lax.ppermute(value, axis, [(i, i ^ by) for i in range(lax.axis_size(axis))])


def pair_lookup(experts, pair_flags, half_axis):
    match = experts[:, None] % half_axis == jnp.arange(half_axis, dtype=jnp.int32)[None, :]
    return jnp.sum(jnp.where(match, pair_flags[None, :], 0), axis=1)


def part_order(parts):
    return (*range(0, parts, 2), *range(1, parts, 2))


def activations_kernel(sources, parts, where_ref, gates_ref, *refs):
    messages = refs[:4]
    gate_ref, up_ref, down_ref = refs[4:7]
    acts_ref, score_ref, keep_ref, give_ref = refs[8:12]
    x_all, dy_all, in_all, down_all, sems = refs[12:]
    rows, width = messages[0].shape
    half = rows // 2
    units = gate_ref.shape[0]
    chunk = width // parts
    copies = []
    for part in range(parts):
        columns = pl.ds(part * chunk, chunk)
        everything = pl.ds(0, units)
        moves = [(gate_ref, everything, in_all, 0, units), (up_ref, everything, in_all, units, units)]
        moves.append((down_ref, everything, down_all, 0, units))
        for i, ref in enumerate(messages):
            moves.append((ref, pl.ds(0, half), x_all, i * half, half))
            moves.append((ref, pl.ds(half, half), dy_all, i * half, half))
        copies.append(
            [
                pltpu.make_async_copy(
                    ref.at[place, columns], target.at[pl.ds(start, size), columns], sems.at[part, i]
                )
                for i, (ref, place, target, start, size) in enumerate(moves)
            ]
        )
        for copy in copies[-1]:
            copy.start()
    me, group = where_ref[0], where_ref[1]
    pre, back = None, None
    for part in range(parts):
        for copy in copies[part]:
            copy.wait()
        columns = pl.ds(part * chunk, chunk)
        one = lax.dot_general(
            in_all[:, columns], x_all[:, columns], CONTRACT_LAST, preferred_element_type=jnp.float32
        )
        two = lax.dot_general(
            down_all[:, columns], dy_all[:, columns], CONTRACT_LAST, preferred_element_type=jnp.float32
        )
        pre = one if pre is None else pre + one
        back = two if back is None else back + two
    pre_gate, pre_up = pre[:units], pre[units:]
    first = lax.broadcasted_iota(jnp.int32, (1, rows), 1) < half
    g = jnp.concatenate(
        [
            jnp.where(first, gates_ref[pl.ds(me ^ one, 1), :], gates_ref[pl.ds(me ^ two, 1), :])
            for one, two in (sources, (sources[0] ^ CORE, sources[1] ^ CORE))
        ],
        axis=1,
    )
    sigma = jax.nn.sigmoid(pre_gate)
    active = pre_gate * sigma
    hidden = active * pre_up
    score_ref[...] = jnp.sum(hidden * back, axis=0, keepdims=True)
    grad_hidden = g * back
    slope = sigma * (1.0 + pre_gate * (1.0 - sigma))
    acts_ref[pl.ds(0, units), :] = (grad_hidden * pre_up * slope).astype(jnp.bfloat16)
    acts_ref[pl.ds(units, units), :] = (grad_hidden * active).astype(jnp.bfloat16)
    acts_ref[pl.ds(2 * units, units), :] = (g * hidden).astype(jnp.bfloat16)
    both = acts_ref[pl.ds(0, 2 * units), :]
    for place, part in enumerate(part_order(parts)):
        columns = pl.ds(pl.multiple_of((group ^ part) * chunk, chunk), chunk)
        share = lax.dot_general(both, in_all[:, columns], CONTRACT_ROWS, preferred_element_type=jnp.float32)
        share = share.astype(jnp.bfloat16)
        keep_ref[place] = share[:rows]
        give_ref[place] = share[rows:]


def activations(sources, parts, where, gates, messages, weights, before):
    rows, width = messages[0].shape
    units = weights[0].shape[0]
    bf16 = jnp.bfloat16
    share = jax.ShapeDtypeStruct((parts, rows, width // parts), bf16)
    return pl.pallas_call(
        functools.partial(activations_kernel, sources, parts),
        out_shape=(
            jax.ShapeDtypeStruct((3 * units, 2 * rows), bf16),
            jax.ShapeDtypeStruct((1, 2 * rows), jnp.float32),
            share,
            share,
        ),
        in_specs=[pl.BlockSpec(memory_space=pltpu.SMEM), pl.BlockSpec(memory_space=pltpu.VMEM)]
        + [pl.BlockSpec(memory_space=pl.ANY)] * 8,
        out_specs=[pl.BlockSpec(memory_space=pltpu.VMEM)] * 4,
        scratch_shapes=[
            pltpu.VMEM((2 * rows, width), bf16),
            pltpu.VMEM((2 * rows, width), bf16),
            pltpu.VMEM((2 * units, width), bf16),
            pltpu.VMEM((units, width), bf16),
            pltpu.SemaphoreType.DMA((parts, 11)),
        ],
        compiler_params=pltpu.CompilerParams(vmem_limit_bytes=VMEM),
        cost_estimate=pl.CostEstimate(flops=1, bytes_accessed=1, transcendentals=0),
        name="activations",
    )(where, gates, *messages, *weights, before)


def weight_grads_kernel(sources, parts, flag_ref, *refs):
    count = 4 * len(sources)
    messages = refs[:count]
    own_ref, other_ref = refs[count : count + 2]
    outs = refs[count + 2 : count + 5]
    x_all, dy_all, acts, sems = refs[count + 5 :]
    rows, width = messages[0].shape
    half = rows // 2
    units = outs[0].shape[1]
    chunk = width // parts
    copies = []
    for part in range(parts):
        columns = pl.ds(part * chunk, chunk)
        copies.append([])
        for i, ref in enumerate(messages):
            for start, target in ((0, x_all), (half, dy_all)):
                copies[-1].append(
                    pltpu.make_async_copy(
                        ref.at[pl.ds(start, half), columns],
                        target.at[pl.ds(i * half, half), columns],
                        sems.at[part, len(copies[-1])],
                    )
                )
        for copy in copies[-1]:
            copy.start()
    tiles = [(one ^ core, two ^ core) for one, two in sources for core in (0, CORE)]
    first = lax.broadcasted_iota(jnp.int32, (1, rows), 1) < half
    for place, (one, two) in enumerate(tiles):
        from_one = [tile[0] for tile in tiles].index(one ^ ACROSS_Y)
        from_two = [tile[1] for tile in tiles].index(two ^ ACROSS_Y)
        arrived = jnp.where(
            first, other_ref[:, pl.ds(from_one * rows, rows)], other_ref[:, pl.ds(from_two * rows, rows)]
        )
        stay = own_ref[:, pl.ds(place * rows, rows)]
        acts[:, pl.ds(place * rows, rows)] = jnp.where(flag_ref[0] == 1, arrived, stay)
    for part in range(parts):
        for copy in copies[part]:
            copy.wait()
        columns = pl.ds(part * chunk, chunk)
        both = jnp.dot(acts[pl.ds(0, 2 * units), :], x_all[:, columns], preferred_element_type=jnp.float32)
        down = jnp.dot(acts[pl.ds(2 * units, units), :], dy_all[:, columns], preferred_element_type=jnp.float32)
        outs[0][0, :, columns] = both[:units].astype(jnp.bfloat16)
        outs[1][0, :, columns] = both[units:].astype(jnp.bfloat16)
        outs[2][0, :, columns] = down.astype(jnp.bfloat16)


def weight_grads(sources, flag, messages, own, other):
    parts = 8
    rows, width = messages[0].shape
    units = own.shape[0] // 3
    total = len(messages) * rows // 2
    bf16 = jnp.bfloat16
    return pl.pallas_call(
        functools.partial(weight_grads_kernel, sources, parts),
        out_shape=(jax.ShapeDtypeStruct((1, units, width), bf16),) * 3,
        in_specs=[pl.BlockSpec(memory_space=pltpu.SMEM)]
        + [pl.BlockSpec(memory_space=pl.ANY)] * len(messages)
        + [pl.BlockSpec(memory_space=pltpu.VMEM)] * 2,
        out_specs=[pl.BlockSpec(memory_space=pltpu.VMEM)] * 3,
        scratch_shapes=[
            pltpu.VMEM((total, width), bf16),
            pltpu.VMEM((total, width), bf16),
            pltpu.VMEM((3 * units, total), bf16),
            pltpu.SemaphoreType.DMA((parts, 2 * len(messages))),
        ],
        compiler_params=pltpu.CompilerParams(vmem_limit_bytes=VMEM),
        cost_estimate=pl.CostEstimate(flops=1, bytes_accessed=1, transcendentals=0),
        name="weight_grads",
    )(flag, *messages, own, other)


CORE, ACROSS_X, ACROSS_Y = 1, 2, 4


def whole_shards(tokens, cotangent, gate_weight, up_weight, down_weight, expert_ids, gates, swap_flags):
    expert_count = lax.axis_size("expert")
    half_axis = expert_count // 2
    me, group = lax.axis_index("expert"), lax.axis_index("dp")
    half = tokens.shape[0] // 2
    parts = lax.axis_size("dp")
    f32, bf16 = jnp.float32, jnp.bfloat16
    own_flag = pair_lookup(jnp.reshape(me, (1,)), swap_flags, half_axis)
    where = jnp.stack([me, group]).astype(jnp.int32)
    weights = (gate_weight[0], up_weight[0], down_weight[0])

    def expert_swap(value, by):
        return swap(value, "expert", by)

    a = {0: jnp.concatenate([tokens[:half], cotangent[:half]])}
    b = {0: jnp.concatenate([tokens[half:], cotangent[half:]])}
    a[2], b[4] = expert_swap(a[0], ACROSS_X), expert_swap(b[0], ACROSS_Y)
    a[4], b[2] = expert_swap(a[0], ACROSS_Y), expert_swap(b[0], ACROSS_X)
    a[1], b[1] = expert_swap(a[0], CORE), expert_swap(b[0], CORE)

    named = expert_ids[:, :, None] == jnp.arange(expert_count, dtype=jnp.int32)[None, None, :]
    table = jnp.sum(jnp.where(named, gates[:, :, None].astype(f32), 0), axis=1)
    gate_rows = lax.all_to_all(table.T, "expert", split_axis=0, concat_axis=0, tiled=True)

    acts, scores, messages = [], [], []

    def work(one, two, before):
        held = [a[one], b[two], a[one ^ CORE], b[two ^ CORE]]
        act, score, keep, give = activations((one, two), parts, where, gate_rows, held, weights, before)
        acts.append(act)
        scores.append(score)
        messages.extend(held)
        return score, keep, expert_swap(give, CORE)

    def near_sum(keep, given):
        far = keep[parts // 2 :] + given[parts // 2 :]
        near = keep[: parts // 2] + given[: parts // 2]
        return near + swap(far, "dp", 1)

    def far_sum(near):
        return near[0].astype(f32) + swap(near[1], "dp", 2).astype(f32)

    done_a, *share_a = work(0, 0, where)
    a[2], b[4], done_a = lax.optimization_barrier((a[2], b[4], done_a))
    a[6], b[6] = expert_swap(a[2], ACROSS_Y), expert_swap(b[4], ACROSS_X)
    a[3], b[5] = expert_swap(a[2], CORE), expert_swap(b[4], CORE)
    done_b, *share_b = work(2, 4, done_a)
    near_a = near_sum(*share_a)
    a[4], b[2], done_b, near_a = lax.optimization_barrier((a[4], b[2], done_b, near_a))
    a[5], b[3] = expert_swap(a[4], CORE), expert_swap(b[2], CORE)
    done_c, *share_c = work(4, 2, done_b)
    total_a, near_b = far_sum(near_a), near_sum(*share_b)
    a[6], b[6], done_c, total_a, near_b = lax.optimization_barrier((a[6], b[6], done_c, total_a, near_b))
    a[7], b[7] = expert_swap(a[6], CORE), expert_swap(b[6], CORE)
    total_b, near_c = far_sum(near_b), near_sum(*share_c)
    _, *share_d = work(6, 6, done_c)
    total_c, total_d = far_sum(near_c), far_sum(near_sum(*share_d))
    totals = (total_a, total_b, total_c, total_d)

    to_x = jnp.concatenate([totals[1][:half], totals[2][half:]]).astype(bf16)
    to_y = jnp.concatenate([totals[2][:half], totals[1][half:]]).astype(bf16)
    input_grad = totals[0] + expert_swap(to_x, ACROSS_X).astype(f32) + expert_swap(to_y, ACROSS_Y).astype(f32)
    input_grad = input_grad + expert_swap(totals[3].astype(bf16), ACROSS_X | ACROSS_Y).astype(f32)

    sources = ((0, 0), (2, 4), (4, 2), (6, 6))
    own = jnp.concatenate(acts, axis=1)
    grads = weight_grads(sources, own_flag, messages, own, expert_swap(own, half_axis))

    tiles = jnp.concatenate(scores, axis=1).reshape(expert_count, 2 * half)
    score_rows = jnp.concatenate(
        [
            tiles[:2],
            jnp.concatenate([tiles[2:6, :half], tiles[jnp.array([4, 5, 2, 3]), half:]], axis=1),
            tiles[6:],
        ]
    )
    summed = score_rows
    for part in range(1, parts):
        summed = summed + swap(score_rows, "dp", part)
    score_rows = jnp.take(summed.astype(bf16), jnp.arange(expert_count, dtype=jnp.int32) ^ me, axis=0)
    score_rows = lax.all_to_all(score_rows, "expert", split_axis=0, concat_axis=0, tiled=True)
    gate_grad = jnp.sum(jnp.where(named, score_rows.T[:, None, :].astype(f32), 0), axis=2)
    return (input_grad.astype(bf16), gate_grad.astype(bf16), *grads)


def packed_shards(tokens, cotangent, gate_weight, up_weight, down_weight, expert_ids, gates, swap_flags):
    expert_count = lax.axis_size("expert")
    half_axis = expert_count // 2
    my_slot = lax.axis_index("expert")
    row_count, model_width = tokens.shape
    routed = expert_ids.shape[1]
    capacity = row_count * routed * 5 // (4 * expert_count)
    groups = lax.axis_size("dp")
    quarter = model_width // groups
    own_flag = pair_lookup(jnp.reshape(my_slot, (1,)), swap_flags, half_axis)[0]
    flat_ids = expert_ids.reshape(-1)
    weights = (gate_weight, up_weight, down_weight)
    arrived = from_behind((gate_weight, up_weight, down_weight), "expert", half_axis)
    weights = tuple(
        (jnp.where(own_flag == 1, fresh, stay) for fresh, stay in zip(arrived, weights))
    )
    flipped = pair_lookup(flat_ids, swap_flags, half_axis)
    target = jnp.where(flipped == 1, (flat_ids + half_axis) % expert_count, flat_ids)
    copies = row_count * routed
    onehot = (target[:, None] == jnp.arange(expert_count, dtype=jnp.int32)[None, :]).astype(
        jnp.int32
    )
    earlier = jnp.cumsum(onehot, axis=0) - onehot
    position = jnp.sum(earlier * onehot, axis=1)
    buffer_index = target * capacity + position
    source = jnp.zeros((expert_count * capacity,), jnp.int32)
    source = source.at[buffer_index].set(jnp.arange(copies, dtype=jnp.int32) + 1)
    filled = source > 0
    copy_index = jnp.maximum(source - 1, 0)
    token_index = copy_index // routed
    x_buffer = jnp.where(filled[:, None], tokens[token_index], 0)
    dy_buffer = jnp.where(filled[:, None], cotangent[token_index], 0)
    gate_buffer = jnp.where(filled, gates.reshape(-1)[copy_index], 0)
    x_rows, dy_rows, gate_rows = (
        lax.all_to_all(x_buffer, "expert", split_axis=0, concat_axis=0, tiled=True),
        lax.all_to_all(dy_buffer, "expert", split_axis=0, concat_axis=0, tiled=True),
        lax.all_to_all(gate_buffer, "expert", split_axis=0, concat_axis=0, tiled=True),
    )
    w_gate = weights[0][0]
    w_up = weights[1][0]
    w_down = weights[2][0]
    contract_last = (((1,), (1,)), ((), ()))
    pre_gate = lax.dot_general(x_rows, w_gate, contract_last, preferred_element_type=jnp.float32)
    pre_up = lax.dot_general(x_rows, w_up, contract_last, preferred_element_type=jnp.float32)
    sigma = jax.nn.sigmoid(pre_gate)
    active = pre_gate * sigma
    hidden = (active * pre_up).astype(jnp.bfloat16)
    back = lax.dot_general(dy_rows, w_down, contract_last, preferred_element_type=jnp.float32)
    score_part = jnp.sum(hidden.astype(jnp.float32) * back, axis=1)
    grad_hidden = gate_rows.astype(jnp.float32)[:, None] * back
    slope = sigma * (1.0 + pre_gate * (1.0 - sigma))
    grad_gate = (grad_hidden * pre_up * slope).astype(jnp.bfloat16)
    grad_up = (grad_hidden * active).astype(jnp.bfloat16)
    input_part = jnp.dot(grad_gate, w_gate, preferred_element_type=jnp.float32)
    input_part = input_part + jnp.dot(grad_up, w_up, preferred_element_type=jnp.float32)
    scaled = gate_rows[:, None] * dy_rows
    contract_rows = (((0,), (0,)), ((), ()))
    grad_wgate = lax.dot_general(
        grad_gate, x_rows, contract_rows, preferred_element_type=jnp.float32
    )
    grad_wup = lax.dot_general(grad_up, x_rows, contract_rows, preferred_element_type=jnp.float32)
    grad_wdown = lax.dot_general(hidden, scaled, contract_rows, preferred_element_type=jnp.float32)
    scores = lax.psum(score_part, "dp")
    input_share = lax.psum_scatter(input_part, "dp", scatter_dimension=1, tiled=True).astype(
        jnp.bfloat16
    )
    back_rows, back_scores = (
        lax.all_to_all(input_share, "expert", split_axis=0, concat_axis=0, tiled=True),
        lax.all_to_all(
            scores.astype(jnp.bfloat16), "expert", split_axis=0, concat_axis=0, tiled=True
        ),
    )
    per_copy = back_rows[buffer_index].reshape(row_count, routed, quarter)
    input_grad = jnp.sum(per_copy.astype(jnp.float32), axis=1).astype(jnp.bfloat16)
    gate_grad = back_scores[buffer_index].reshape(row_count, routed)
    gradients = (
        grad_wgate.astype(jnp.bfloat16)[None],
        grad_wup.astype(jnp.bfloat16)[None],
        grad_wdown.astype(jnp.bfloat16)[None],
    )
    return (input_grad, gate_grad, gradients[0], gradients[1], gradients[2])


def chosen(tokens, cotangent, gate_weight, up_weight, down_weight, expert_ids, gates, swap_flags):
    capacity = tokens.shape[0] * expert_ids.shape[1] * 5 // (4 * lax.axis_size("expert"))
    body = whole_shards if 2 * capacity >= tokens.shape[0] else packed_shards
    return body(tokens, cotangent, gate_weight, up_weight, down_weight, expert_ids, gates, swap_flags)


def solution(mesh):
    placed = (
        P("expert", None),
        P("expert", None),
        P("expert", "dp", None),
        P("expert", "dp", None),
        P("expert", "dp", None),
        P("expert", None),
        P("expert", None),
        P(),
    )
    return jax.shard_map(
        chosen,
        mesh=mesh,
        in_specs=placed,
        out_specs=(
            P("expert", "dp"),
            P("expert", None),
            P("expert", "dp", None),
            P("expert", "dp", None),
            P("expert", "dp", None),
        ),
        check_vma=False,
    )
```

```python
import functools

import jax
import jax.numpy as jnp
from jax import lax
from jax.experimental import pallas as pl
from jax.experimental.pallas import tpu as pltpu
from jax.sharding import PartitionSpec as P


CONTRACT_LAST = (((1,), (1,)), ((), ()))
CONTRACT_ROWS = (((0,), (0,)), ((), ()))
VMEM = 56 * 1024 * 1024


def from_behind(value, axis, by):
    devices = lax.axis_size(axis)
    return lax.ppermute(value, axis, [(i, (i + by) % devices) for i in range(devices)])


def swap(value, axis, by):
    return lax.ppermute(value, axis, [(i, i ^ by) for i in range(lax.axis_size(axis))])


def pair_lookup(experts, pair_flags, half_axis):
    match = experts[:, None] % half_axis == jnp.arange(half_axis, dtype=jnp.int32)[None, :]
    return jnp.sum(jnp.where(match, pair_flags[None, :], 0), axis=1)


def part_order(parts):
    return (*range(0, parts, 2), *range(1, parts, 2))


def activations_kernel(parts, where_ref, one_ref, two_ref, *refs):
    messages = refs[:4]
    gate_ref, up_ref, down_ref = refs[4:7]
    acts_ref, score_ref, keep_ref, give_ref = refs[8:12]
    held, in_all, down_all, both, shares, sems, out_sems = refs[12:]
    rows, width = messages[0].shape
    half = rows // 2
    units = gate_ref.shape[0]
    chunk = width // parts
    copies = []
    for part in range(parts):
        columns = pl.ds(part * chunk, chunk)
        moves = [(ref, held.at[i, :, columns]) for i, ref in enumerate(messages)]
        moves.append((gate_ref, in_all.at[pl.ds(0, units), columns]))
        moves.append((up_ref, in_all.at[pl.ds(units, units), columns]))
        moves.append((down_ref, down_all.at[:, columns]))
        copies.append(
            [
                pltpu.make_async_copy(ref.at[:, columns], target, sems.at[part, i])
                for i, (ref, target) in enumerate(moves)
            ]
        )
        for copy in copies[-1]:
            copy.start()
    me, group = where_ref[0], where_ref[1]
    first = lax.broadcasted_iota(jnp.int32, (1, rows), 1) < half
    experts = one_ref.shape[0] // 2
    g = jnp.concatenate(
        [
            jnp.where(first, one_ref[pl.ds(me + core, 1), :], two_ref[pl.ds(me + core, 1), :])
            for core in (0, experts)
        ],
        axis=1,
    )
    pre, back = None, None
    for part in range(parts):
        for copy in copies[part]:
            copy.wait()
        columns = pl.ds(part * chunk, chunk)
        x = held[:, pl.ds(0, half), columns].reshape(2 * rows, chunk)
        dy = held[:, pl.ds(half, half), columns].reshape(2 * rows, chunk)
        one = lax.dot_general(in_all[:, columns], x, CONTRACT_LAST, preferred_element_type=jnp.float32)
        two = lax.dot_general(down_all[:, columns], dy, CONTRACT_LAST, preferred_element_type=jnp.float32)
        pre = one if pre is None else pre + one
        back = two if back is None else back + two
    pre_gate, pre_up = pre[:units], pre[units:]
    sigma = jax.nn.sigmoid(pre_gate)
    active = pre_gate * sigma
    hidden = active * pre_up
    score_ref[...] = jnp.sum(hidden * back, axis=0, keepdims=True)
    grad_hidden = g * back
    slope = sigma * (1.0 + pre_gate * (1.0 - sigma))
    grads = jnp.concatenate([grad_hidden * pre_up * slope, grad_hidden * active], axis=0)
    acts_ref[pl.ds(0, 2 * units), :] = grads.astype(jnp.bfloat16)
    acts_ref[pl.ds(2 * units, units), :] = (g * hidden).astype(jnp.bfloat16)
    both[...] = grads.T.astype(jnp.bfloat16)
    copies = []
    for place, part in enumerate(part_order(parts)):
        columns = pl.ds(pl.multiple_of((group ^ part) * chunk, chunk), chunk)
        share = jnp.dot(both[...], in_all[:, columns], preferred_element_type=jnp.float32)
        shares[place] = share.astype(jnp.bfloat16)
        for i, ref in enumerate((keep_ref, give_ref)):
            copies.append(
                pltpu.make_async_copy(
                    shares.at[place, pl.ds(i * rows, rows), :], ref.at[place], out_sems.at[place, i]
                )
            )
            copies[-1].start()
    for copy in copies:
        copy.wait()


def activations(parts, where, tables, messages, weights, before):
    rows, width = messages[0].shape
    units = weights[0].shape[0]
    bf16 = jnp.bfloat16
    share = jax.ShapeDtypeStruct((parts, rows, width // parts), bf16)
    return pl.pallas_call(
        functools.partial(activations_kernel, parts),
        out_shape=(
            jax.ShapeDtypeStruct((3 * units, 2 * rows), bf16),
            jax.ShapeDtypeStruct((1, 2 * rows), jnp.float32),
            share,
            share,
        ),
        in_specs=[pl.BlockSpec(memory_space=pltpu.SMEM)]
        + [pl.BlockSpec(memory_space=pltpu.VMEM)] * 2
        + [pl.BlockSpec(memory_space=pl.ANY)] * 8,
        out_specs=[pl.BlockSpec(memory_space=pltpu.VMEM)] * 2 + [pl.BlockSpec(memory_space=pl.ANY)] * 2,
        scratch_shapes=[
            pltpu.VMEM((4, rows, width), bf16),
            pltpu.VMEM((2 * units, width), bf16),
            pltpu.VMEM((units, width), bf16),
            pltpu.VMEM((2 * rows, 2 * units), bf16),
            pltpu.VMEM((parts, 2 * rows, width // parts), bf16),
            pltpu.SemaphoreType.DMA((parts, 7)),
            pltpu.SemaphoreType.DMA((parts, 2)),
        ],
        compiler_params=pltpu.CompilerParams(vmem_limit_bytes=VMEM),
        cost_estimate=pl.CostEstimate(flops=1, bytes_accessed=1, transcendentals=0),
        name="activations",
    )(where, *tables, *messages, *weights, before)


def weight_grads_kernel(sources, parts, flag_ref, *refs):
    count = 4 * len(sources)
    messages = refs[:count]
    own_ref, other_ref = refs[count : count + 2]
    outs = refs[count + 2 : count + 5]
    held, acts, results, sems, out_sems = refs[count + 5 :]
    rows, width = messages[0].shape
    half = rows // 2
    units = outs[0].shape[1]
    chunk = width // parts
    copies = []
    for part in range(parts):
        columns = pl.ds(part * chunk, chunk)
        copies.append(
            [
                pltpu.make_async_copy(ref.at[:, columns], held.at[i, :, columns], sems.at[part, i])
                for i, ref in enumerate(messages)
            ]
        )
        for copy in copies[-1]:
            copy.start()
    tiles = [(one ^ core, two ^ core) for one, two in sources for core in (0, CORE)]
    first = lax.broadcasted_iota(jnp.int32, (1, rows), 1) < half
    for place, (one, two) in enumerate(tiles):
        from_one = [tile[0] for tile in tiles].index(one ^ ACROSS_Y)
        from_two = [tile[1] for tile in tiles].index(two ^ ACROSS_Y)
        arrived = jnp.where(
            first, other_ref[:, pl.ds(from_one * rows, rows)], other_ref[:, pl.ds(from_two * rows, rows)]
        )
        stay = own_ref[:, pl.ds(place * rows, rows)]
        acts[:, pl.ds(place * rows, rows)] = jnp.where(flag_ref[0] == 1, arrived, stay)
    sent = []
    for part in range(parts):
        for copy in copies[part]:
            copy.wait()
        columns = pl.ds(part * chunk, chunk)
        x = held[:, pl.ds(0, half), columns].reshape(count * half, chunk)
        dy = held[:, pl.ds(half, half), columns].reshape(count * half, chunk)
        both = jnp.dot(acts[pl.ds(0, 2 * units), :], x, preferred_element_type=jnp.float32)
        results[part, pl.ds(0, 2 * units), :] = both.astype(jnp.bfloat16)
        down = jnp.dot(acts[pl.ds(2 * units, units), :], dy, preferred_element_type=jnp.float32)
        results[part, pl.ds(2 * units, units), :] = down.astype(jnp.bfloat16)
        for i, out in enumerate(outs):
            sent.append(
                pltpu.make_async_copy(
                    results.at[part, pl.ds(i * units, units), :], out.at[0, :, columns], out_sems.at[part, i]
                )
            )
            sent[-1].start()
    for copy in sent:
        copy.wait()


def weight_grads(sources, flag, messages, own, other):
    parts = 4
    rows, width = messages[0].shape
    units = own.shape[0] // 3
    total = len(messages) * rows // 2
    bf16 = jnp.bfloat16
    return pl.pallas_call(
        functools.partial(weight_grads_kernel, sources, parts),
        out_shape=(jax.ShapeDtypeStruct((1, units, width), bf16),) * 3,
        in_specs=[pl.BlockSpec(memory_space=pltpu.SMEM)]
        + [pl.BlockSpec(memory_space=pl.ANY)] * len(messages)
        + [pl.BlockSpec(memory_space=pltpu.VMEM)] * 2,
        out_specs=[pl.BlockSpec(memory_space=pl.ANY)] * 3,
        scratch_shapes=[
            pltpu.VMEM((len(messages), rows, width), bf16),
            pltpu.VMEM((3 * units, total), bf16),
            pltpu.VMEM((parts, 3 * units, width // parts), bf16),
            pltpu.SemaphoreType.DMA((parts, len(messages))),
            pltpu.SemaphoreType.DMA((parts, 3)),
        ],
        compiler_params=pltpu.CompilerParams(vmem_limit_bytes=VMEM),
        cost_estimate=pl.CostEstimate(flops=1, bytes_accessed=1, transcendentals=0),
        name="weight_grads",
    )(flag, *messages, own, other)


CORE, ACROSS_X, ACROSS_Y = 1, 2, 4


def whole_shards(tokens, cotangent, gate_weight, up_weight, down_weight, expert_ids, gates, swap_flags):
    expert_count = lax.axis_size("expert")
    half_axis = expert_count // 2
    me, group = lax.axis_index("expert"), lax.axis_index("dp")
    half = tokens.shape[0] // 2
    parts = lax.axis_size("dp")
    f32, bf16 = jnp.float32, jnp.bfloat16
    own_flag = pair_lookup(jnp.reshape(me, (1,)), swap_flags, half_axis)
    where = jnp.stack([me, group]).astype(jnp.int32)
    weights = (gate_weight[0], up_weight[0], down_weight[0])

    def expert_swap(value, by):
        return swap(value, "expert", by)

    a = {0: jnp.concatenate([tokens[:half], cotangent[:half]])}
    b = {0: jnp.concatenate([tokens[half:], cotangent[half:]])}
    a[2], b[4] = expert_swap(a[0], ACROSS_X), expert_swap(b[0], ACROSS_Y)
    a[4], b[2] = expert_swap(a[0], ACROSS_Y), expert_swap(b[0], ACROSS_X)
    a[1], b[1] = expert_swap(a[0], CORE), expert_swap(b[0], CORE)

    named = expert_ids[:, :, None] == jnp.arange(expert_count, dtype=jnp.int32)[None, None, :]
    table = jnp.sum(jnp.where(named, gates[:, :, None].astype(f32), 0), axis=1)
    tables = {0: jnp.concatenate([table.T, expert_swap(table.T, CORE)])}
    tables[2], tables[4] = expert_swap(tables[0], ACROSS_X), expert_swap(tables[0], ACROSS_Y)

    acts, scores, messages = [], [], []

    def work(one, two, before):
        held = [a[one], b[two], a[one ^ CORE], b[two ^ CORE]]
        act, score, keep, give = activations(
            parts, where, (tables[one], tables[two]), held, weights, before
        )
        acts.append(act)
        scores.append(score)
        messages.extend(held)
        return score, keep, expert_swap(give, CORE)

    def to_neighbour(keep, given):
        far = keep[parts // 2 :] + given[parts // 2 :]
        return keep[: parts // 2] + given[: parts // 2], swap(far, "dp", 1)

    def to_far(near, arrived):
        near = near + arrived
        return near[0].astype(f32), swap(near[1], "dp", 2)

    barrier = lax.optimization_barrier

    done_a, *share_a = work(0, 0, where)
    a[2], b[4], tables[2], tables[4], done_a = barrier((a[2], b[4], tables[2], tables[4], done_a))
    a[6], b[6] = expert_swap(a[2], ACROSS_Y), expert_swap(b[4], ACROSS_X)
    tables[6] = expert_swap(tables[2], ACROSS_Y)
    a[3], b[5] = expert_swap(a[2], CORE), expert_swap(b[4], CORE)
    done_b, *share_b = work(2, 4, done_a)
    near_a, near_in_a = to_neighbour(*share_a)
    a[4], b[2], done_b, near_in_a = barrier((a[4], b[2], done_b, near_in_a))
    a[5], b[3] = expert_swap(a[4], CORE), expert_swap(b[2], CORE)
    done_c, *share_c = work(4, 2, done_b)
    total_a, far_in_a = to_far(near_a, near_in_a)
    near_b, near_in_b = to_neighbour(*share_b)
    a[6], b[6], done_c, far_in_a, near_in_b = barrier((a[6], b[6], done_c, far_in_a, near_in_b))
    a[7], b[7] = expert_swap(a[6], CORE), expert_swap(b[6], CORE)
    done_d, *share_d = work(6, 6, done_c)
    total_b, far_in_b = to_far(near_b, near_in_b)
    near_c, near_in_c = to_neighbour(*share_c)
    done_d, far_in_b, near_in_c = barrier((done_d, far_in_b, near_in_c))
    scores[-1] = done_d
    total_c, far_in_c = to_far(near_c, near_in_c)
    near_d, near_in_d = to_neighbour(*share_d)

    sources = ((0, 0), (2, 4), (4, 2), (6, 6))
    own = jnp.concatenate(acts, axis=1)
    other = expert_swap(own, half_axis)

    tiles = jnp.concatenate(scores, axis=1).reshape(expert_count, 2 * half)
    second = jnp.concatenate([tiles[:2, half:], tiles[4:6, half:], tiles[2:4, half:], tiles[6:, half:]])
    score_rows = jnp.concatenate([tiles[:, :half], second], axis=1)
    summed = score_rows + swap(score_rows, "dp", 1)
    summed, near_in_d, far_in_c = barrier((summed, near_in_d, far_in_c))
    summed = summed + swap(summed, "dp", 2)
    score_rows = jnp.take(summed.astype(bf16), jnp.arange(expert_count, dtype=jnp.int32) ^ me, axis=0)
    score_rows = lax.all_to_all(score_rows, "expert", split_axis=0, concat_axis=0, tiled=True)
    total_d, far_in_d = to_far(near_d, near_in_d)
    score_rows, far_in_d, own_flag = barrier((score_rows, far_in_d, own_flag))
    total_a, total_b = total_a + far_in_a.astype(f32), total_b + far_in_b.astype(f32)
    total_c, total_d = total_c + far_in_c.astype(f32), (total_d + far_in_d.astype(f32)).astype(bf16)
    grads = weight_grads(sources, own_flag, messages, own, other)

    to_x = jnp.concatenate([total_b[:half], total_c[half:]]).astype(bf16)
    to_y = jnp.concatenate([total_c[:half], total_b[half:]]).astype(bf16)
    input_grad = total_a + expert_swap(to_x, ACROSS_X).astype(f32) + expert_swap(to_y, ACROSS_Y).astype(f32)
    input_grad = input_grad + expert_swap(total_d, ACROSS_X | ACROSS_Y).astype(f32)
    gate_grad = jnp.sum(jnp.where(named, score_rows.T[:, None, :].astype(f32), 0), axis=2)
    return (input_grad.astype(bf16), gate_grad.astype(bf16), *grads)


def packed_shards(tokens, cotangent, gate_weight, up_weight, down_weight, expert_ids, gates, swap_flags):
    expert_count = lax.axis_size("expert")
    half_axis = expert_count // 2
    my_slot = lax.axis_index("expert")
    row_count, model_width = tokens.shape
    routed = expert_ids.shape[1]
    capacity = row_count * routed * 5 // (4 * expert_count)
    groups = lax.axis_size("dp")
    quarter = model_width // groups
    own_flag = pair_lookup(jnp.reshape(my_slot, (1,)), swap_flags, half_axis)[0]
    flat_ids = expert_ids.reshape(-1)
    weights = (gate_weight, up_weight, down_weight)
    arrived = from_behind((gate_weight, up_weight, down_weight), "expert", half_axis)
    weights = tuple(
        (jnp.where(own_flag == 1, fresh, stay) for fresh, stay in zip(arrived, weights))
    )
    flipped = pair_lookup(flat_ids, swap_flags, half_axis)
    target = jnp.where(flipped == 1, (flat_ids + half_axis) % expert_count, flat_ids)
    copies = row_count * routed
    onehot = (target[:, None] == jnp.arange(expert_count, dtype=jnp.int32)[None, :]).astype(
        jnp.int32
    )
    earlier = jnp.cumsum(onehot, axis=0) - onehot
    position = jnp.sum(earlier * onehot, axis=1)
    buffer_index = target * capacity + position
    source = jnp.zeros((expert_count * capacity,), jnp.int32)
    source = source.at[buffer_index].set(jnp.arange(copies, dtype=jnp.int32) + 1)
    filled = source > 0
    copy_index = jnp.maximum(source - 1, 0)
    token_index = copy_index // routed
    x_buffer = jnp.where(filled[:, None], tokens[token_index], 0)
    dy_buffer = jnp.where(filled[:, None], cotangent[token_index], 0)
    gate_buffer = jnp.where(filled, gates.reshape(-1)[copy_index], 0)
    x_rows, dy_rows, gate_rows = (
        lax.all_to_all(x_buffer, "expert", split_axis=0, concat_axis=0, tiled=True),
        lax.all_to_all(dy_buffer, "expert", split_axis=0, concat_axis=0, tiled=True),
        lax.all_to_all(gate_buffer, "expert", split_axis=0, concat_axis=0, tiled=True),
    )
    w_gate = weights[0][0]
    w_up = weights[1][0]
    w_down = weights[2][0]
    contract_last = (((1,), (1,)), ((), ()))
    pre_gate = lax.dot_general(x_rows, w_gate, contract_last, preferred_element_type=jnp.float32)
    pre_up = lax.dot_general(x_rows, w_up, contract_last, preferred_element_type=jnp.float32)
    sigma = jax.nn.sigmoid(pre_gate)
    active = pre_gate * sigma
    hidden = (active * pre_up).astype(jnp.bfloat16)
    back = lax.dot_general(dy_rows, w_down, contract_last, preferred_element_type=jnp.float32)
    score_part = jnp.sum(hidden.astype(jnp.float32) * back, axis=1)
    grad_hidden = gate_rows.astype(jnp.float32)[:, None] * back
    slope = sigma * (1.0 + pre_gate * (1.0 - sigma))
    grad_gate = (grad_hidden * pre_up * slope).astype(jnp.bfloat16)
    grad_up = (grad_hidden * active).astype(jnp.bfloat16)
    input_part = jnp.dot(grad_gate, w_gate, preferred_element_type=jnp.float32)
    input_part = input_part + jnp.dot(grad_up, w_up, preferred_element_type=jnp.float32)
    scaled = gate_rows[:, None] * dy_rows
    contract_rows = (((0,), (0,)), ((), ()))
    grad_wgate = lax.dot_general(
        grad_gate, x_rows, contract_rows, preferred_element_type=jnp.float32
    )
    grad_wup = lax.dot_general(grad_up, x_rows, contract_rows, preferred_element_type=jnp.float32)
    grad_wdown = lax.dot_general(hidden, scaled, contract_rows, preferred_element_type=jnp.float32)
    scores = lax.psum(score_part, "dp")
    input_share = lax.psum_scatter(input_part, "dp", scatter_dimension=1, tiled=True).astype(
        jnp.bfloat16
    )
    back_rows, back_scores = (
        lax.all_to_all(input_share, "expert", split_axis=0, concat_axis=0, tiled=True),
        lax.all_to_all(
            scores.astype(jnp.bfloat16), "expert", split_axis=0, concat_axis=0, tiled=True
        ),
    )
    per_copy = back_rows[buffer_index].reshape(row_count, routed, quarter)
    input_grad = jnp.sum(per_copy.astype(jnp.float32), axis=1).astype(jnp.bfloat16)
    gate_grad = back_scores[buffer_index].reshape(row_count, routed)
    gradients = (
        grad_wgate.astype(jnp.bfloat16)[None],
        grad_wup.astype(jnp.bfloat16)[None],
        grad_wdown.astype(jnp.bfloat16)[None],
    )
    return (input_grad, gate_grad, gradients[0], gradients[1], gradients[2])


def chosen(tokens, cotangent, gate_weight, up_weight, down_weight, expert_ids, gates, swap_flags):
    capacity = tokens.shape[0] * expert_ids.shape[1] * 5 // (4 * lax.axis_size("expert"))
    body = whole_shards if 2 * capacity >= tokens.shape[0] else packed_shards
    return body(tokens, cotangent, gate_weight, up_weight, down_weight, expert_ids, gates, swap_flags)


def solution(mesh):
    placed = (
        P("expert", None),
        P("expert", None),
        P("expert", "dp", None),
        P("expert", "dp", None),
        P("expert", "dp", None),
        P("expert", None),
        P("expert", None),
        P(),
    )
    return jax.shard_map(
        chosen,
        mesh=mesh,
        in_specs=placed,
        out_specs=(
            P("expert", "dp"),
            P("expert", None),
            P("expert", "dp", None),
            P("expert", "dp", None),
            P("expert", "dp", None),
        ),
        check_vma=False,
    )
```

```python
import functools

import jax
import jax.numpy as jnp
from jax import lax
from jax.experimental import pallas as pl
from jax.experimental.pallas import tpu as pltpu
from jax.sharding import PartitionSpec as P


CONTRACT_LAST = (((1,), (1,)), ((), ()))
CONTRACT_ROWS = (((0,), (0,)), ((), ()))
VMEM = 20 * 1024 * 1024


def from_behind(value, axis, by):
    devices = lax.axis_size(axis)
    return lax.ppermute(value, axis, [(i, (i + by) % devices) for i in range(devices)])


def swap(value, axis, by):
    return lax.ppermute(value, axis, [(i, i ^ by) for i in range(lax.axis_size(axis))])


def pair_lookup(experts, pair_flags, half_axis):
    match = experts[:, None] % half_axis == jnp.arange(half_axis, dtype=jnp.int32)[None, :]
    return jnp.sum(jnp.where(match, pair_flags[None, :], 0), axis=1)


def in_vmem(*values):
    return [pltpu.with_memory_space_constraint(value, pltpu.VMEM) for value in values]


def rows_of(messages, start, size, columns):
    return jnp.concatenate([ref[pl.ds(start, size), columns] for ref in messages], axis=0)


def activations_kernel(parts, where_ref, one_ref, two_ref, *refs):
    messages = refs[:4]
    in_ref, down_ref = refs[4:6]
    acts_ref, score_ref, keep_near, keep_far, give_near, give_far, both = refs[7:]
    rows, width = messages[0].shape
    half = rows // 2
    units = down_ref.shape[0]
    chunk = width // parts
    me, group = where_ref[0], where_ref[1]
    first = lax.broadcasted_iota(jnp.int32, (1, rows), 1) < half
    experts = one_ref.shape[0] // 2
    g = jnp.concatenate(
        [
            jnp.where(first, one_ref[pl.ds(me + core, 1), :], two_ref[pl.ds(me + core, 1), :])
            for core in (0, experts)
        ],
        axis=1,
    )
    pre, back = None, None
    for part in range(parts):
        columns = pl.ds(part * chunk, chunk)
        x, dy = rows_of(messages, 0, half, columns), rows_of(messages, half, half, columns)
        one = lax.dot_general(in_ref[:, columns], x, CONTRACT_LAST, preferred_element_type=jnp.float32)
        two = lax.dot_general(down_ref[:, columns], dy, CONTRACT_LAST, preferred_element_type=jnp.float32)
        pre = one if pre is None else pre + one
        back = two if back is None else back + two
    pre_gate, pre_up = pre[:units], pre[units:]
    sigma = jax.nn.sigmoid(pre_gate)
    active = pre_gate * sigma
    hidden = active * pre_up
    score_ref[...] = jnp.sum(hidden * back, axis=0, keepdims=True)
    grad_hidden = g * back
    slope = sigma * (1.0 + pre_gate * (1.0 - sigma))
    grads = jnp.concatenate([grad_hidden * pre_up * slope, grad_hidden * active], axis=0)
    acts_ref[pl.ds(0, 2 * units), :] = grads.astype(jnp.bfloat16)
    acts_ref[pl.ds(2 * units, units), :] = (g * hidden).astype(jnp.bfloat16)
    both[...] = grads.T.astype(jnp.bfloat16)
    for part in range(parts):
        columns = pl.ds(pl.multiple_of((group ^ part) * chunk, chunk), chunk)
        share = jnp.dot(both[...], in_ref[:, columns], preferred_element_type=jnp.float32)
        share = share.astype(jnp.bfloat16)
        keep, give = (keep_far, give_far) if part % 2 else (keep_near, give_near)
        keep[part // 2] = share[:rows]
        give[part // 2] = share[rows:]


def activations(parts, where, tables, messages, weights, before):
    rows, width = messages[0].shape
    units = weights[1].shape[0]
    bf16 = jnp.bfloat16
    share = pltpu.VMEM((parts // 2, rows, width // parts), bf16)
    return pl.pallas_call(
        functools.partial(activations_kernel, parts),
        out_shape=(
            pltpu.VMEM((3 * units, 2 * rows), bf16),
            pltpu.VMEM((1, 2 * rows), jnp.float32),
            share,
            share,
            share,
            share,
        ),
        in_specs=[pl.BlockSpec(memory_space=pltpu.SMEM)]
        + [pl.BlockSpec(memory_space=pltpu.VMEM)] * 8
        + [pl.BlockSpec(memory_space=pl.ANY)],
        out_specs=[pl.BlockSpec(memory_space=pltpu.VMEM)] * 6,
        scratch_shapes=[pltpu.VMEM((2 * rows, 2 * units), bf16)],
        compiler_params=pltpu.CompilerParams(vmem_limit_bytes=VMEM),
        cost_estimate=pl.CostEstimate(flops=1, bytes_accessed=1, transcendentals=0),
        name="activations",
    )(where, *in_vmem(*tables, *messages, *weights), before)


def weight_grads_kernel(sources, parts, flag_ref, *refs):
    groups = len(sources)
    messages, refs = refs[: 4 * groups], refs[4 * groups :]
    own, other, refs = refs[:groups], refs[groups : 2 * groups], refs[2 * groups :]
    outs = refs[:3]
    acts, results, out_sems = refs[3:]
    rows, width = messages[0].shape
    half = rows // 2
    units = outs[0].shape[1]
    chunk = width // parts
    tiles = [(one ^ core, two ^ core) for one, two in sources for core in (0, CORE)]
    first = lax.broadcasted_iota(jnp.int32, (1, rows), 1) < half

    def tile_of(groups_of, place):
        return groups_of[place // 2][:, pl.ds(place % 2 * rows, rows)]

    for place, (one, two) in enumerate(tiles):
        from_one = [tile[0] for tile in tiles].index(one ^ ACROSS_Y)
        from_two = [tile[1] for tile in tiles].index(two ^ ACROSS_Y)
        arrived = jnp.where(first, tile_of(other, from_one), tile_of(other, from_two))
        acts[:, pl.ds(place * rows, rows)] = jnp.where(flag_ref[0] == 1, arrived, tile_of(own, place))
    sent = []
    for part in range(parts):
        columns = pl.ds(part * chunk, chunk)
        x, dy = rows_of(messages, 0, half, columns), rows_of(messages, half, half, columns)
        both = jnp.dot(acts[pl.ds(0, 2 * units), :], x, preferred_element_type=jnp.float32)
        results[part, pl.ds(0, 2 * units), :] = both.astype(jnp.bfloat16)
        down = jnp.dot(acts[pl.ds(2 * units, units), :], dy, preferred_element_type=jnp.float32)
        results[part, pl.ds(2 * units, units), :] = down.astype(jnp.bfloat16)
        for i, out in enumerate(outs):
            sent.append(
                pltpu.make_async_copy(
                    results.at[part, pl.ds(i * units, units), :], out.at[0, :, columns], out_sems.at[part, i]
                )
            )
            sent[-1].start()
    for copy in sent:
        copy.wait()


def weight_grads(sources, flag, messages, own, other):
    parts = 8
    rows, width = messages[0].shape
    units = own[0].shape[0] // 3
    total = len(messages) * rows // 2
    bf16 = jnp.bfloat16
    operands = in_vmem(*messages, *own, *other)
    return pl.pallas_call(
        functools.partial(weight_grads_kernel, sources, parts),
        out_shape=(jax.ShapeDtypeStruct((1, units, width), bf16),) * 3,
        in_specs=[pl.BlockSpec(memory_space=pltpu.SMEM)] + [pl.BlockSpec(memory_space=pltpu.VMEM)] * len(operands),
        out_specs=[pl.BlockSpec(memory_space=pl.ANY)] * 3,
        scratch_shapes=[
            pltpu.VMEM((3 * units, total), bf16),
            pltpu.VMEM((parts, 3 * units, width // parts), bf16),
            pltpu.SemaphoreType.DMA((parts, 3)),
        ],
        compiler_params=pltpu.CompilerParams(vmem_limit_bytes=VMEM),
        cost_estimate=pl.CostEstimate(flops=1, bytes_accessed=1, transcendentals=0),
        name="weight_grads",
    )(flag, *operands)


CORE, ACROSS_X, ACROSS_Y = 1, 2, 4


def whole_shards(tokens, cotangent, gate_weight, up_weight, down_weight, expert_ids, gates, swap_flags):
    expert_count = lax.axis_size("expert")
    half_axis = expert_count // 2
    me, group = lax.axis_index("expert"), lax.axis_index("dp")
    half = tokens.shape[0] // 2
    parts = lax.axis_size("dp")
    f32, bf16 = jnp.float32, jnp.bfloat16
    own_flag = pair_lookup(jnp.reshape(me, (1,)), swap_flags, half_axis)
    where = jnp.stack([me, group]).astype(jnp.int32)
    weights = (jnp.concatenate([gate_weight[0], up_weight[0]]), down_weight[0])

    def expert_swap(value, by):
        return swap(value, "expert", by)

    a = {0: jnp.concatenate([tokens[:half], cotangent[:half]])}
    b = {0: jnp.concatenate([tokens[half:], cotangent[half:]])}
    a[2], b[4] = expert_swap(a[0], ACROSS_X), expert_swap(b[0], ACROSS_Y)
    a[4], b[2] = expert_swap(a[0], ACROSS_Y), expert_swap(b[0], ACROSS_X)
    a[1], b[1] = expert_swap(a[0], CORE), expert_swap(b[0], CORE)

    named = expert_ids[:, :, None] == jnp.arange(expert_count, dtype=jnp.int32)[None, None, :]
    table = jnp.sum(jnp.where(named, gates[:, :, None].astype(f32), 0), axis=1)
    tables = {0: jnp.concatenate([table.T, expert_swap(table.T, CORE)])}
    tables[2], tables[4] = expert_swap(tables[0], ACROSS_X), expert_swap(tables[0], ACROSS_Y)

    acts, scores, messages = [], [], []
    barrier = lax.optimization_barrier

    def work(one, two, before):
        held = [a[one], b[two], a[one ^ CORE], b[two ^ CORE]]
        act, score, keep_near, keep_far, give_near, give_far = activations(
            parts, where, (tables[one], tables[two]), held, weights, before
        )
        acts.append(act)
        scores.append(score)
        messages.extend(held)
        return score, keep_near, keep_far, expert_swap(give_near, CORE), expert_swap(give_far, CORE)

    def to_neighbour(keep_near, keep_far, near, far):
        return keep_near + near, swap(keep_far + far, "dp", 1)

    def to_far(near, arrived):
        near = near + arrived
        return near[0].astype(f32), swap(near[1], "dp", 2)

    done_a, *share_a = work(0, 0, where)
    a[2], b[4], tables[2], tables[4], done_a = barrier((a[2], b[4], tables[2], tables[4], done_a))
    a[6], b[6] = expert_swap(a[2], ACROSS_Y), expert_swap(b[4], ACROSS_X)
    tables[6] = expert_swap(tables[2], ACROSS_Y)
    a[3], b[5] = expert_swap(a[2], CORE), expert_swap(b[4], CORE)
    done_b, *share_b = work(2, 4, done_a)
    near_a, near_in_a = to_neighbour(*share_a)
    a[4], b[2], done_b, near_in_a = barrier((a[4], b[2], done_b, near_in_a))
    a[5], b[3] = expert_swap(a[4], CORE), expert_swap(b[2], CORE)
    done_c, *share_c = work(4, 2, done_b)
    total_a, far_in_a = to_far(near_a, near_in_a)
    near_b, near_in_b = to_neighbour(*share_b)
    a[6], b[6], done_c, far_in_a, near_in_b = barrier((a[6], b[6], done_c, far_in_a, near_in_b))
    a[7], b[7] = expert_swap(a[6], CORE), expert_swap(b[6], CORE)
    other = [expert_swap(act, half_axis) for act in acts[:2]]
    done_d, *share_d = work(6, 6, done_c)
    total_b, far_in_b = to_far(near_b, near_in_b)
    near_c, near_in_c = to_neighbour(*share_c)
    done_d, far_in_b, near_in_c, *other = barrier((done_d, far_in_b, near_in_c, *other))
    other += [expert_swap(act, half_axis) for act in acts[2:]]
    tiles = jnp.concatenate(scores[:3] + [done_d], axis=1).reshape(expert_count, 2 * half)
    second = jnp.concatenate([tiles[:2, half:], tiles[4:6, half:], tiles[2:4, half:], tiles[6:, half:]])
    score_rows = jnp.concatenate([tiles[:, :half], second], axis=1)
    score_in = swap(score_rows, "dp", 1)
    keep_near, keep_far, near, far = share_d
    far, score_in = barrier((far, score_in))
    near_d, near_in_d = to_neighbour(keep_near, keep_far, near, far)
    score_rows = score_rows + score_in
    score_rows = score_rows + swap(score_rows, "dp", 2)
    score_rows = jnp.take(score_rows.astype(bf16), jnp.arange(expert_count, dtype=jnp.int32) ^ me, axis=0)
    score_rows = lax.all_to_all(score_rows, "expert", split_axis=0, concat_axis=0, tiled=True)
    total_c, far_in_c = to_far(near_c, near_in_c)
    score_rows, near_in_d, far_in_c, own_flag = barrier((score_rows, near_in_d, far_in_c, own_flag))
    total_d, far_in_d = to_far(near_d, near_in_d)
    grads = weight_grads(((0, 0), (2, 4), (4, 2), (6, 6)), own_flag, messages, acts, other)
    far_in_d, grads = barrier((far_in_d, grads))

    total_a, total_b = total_a + far_in_a.astype(f32), total_b + far_in_b.astype(f32)
    total_c, total_d = total_c + far_in_c.astype(f32), (total_d + far_in_d.astype(f32)).astype(bf16)
    to_x = jnp.concatenate([total_b[:half], total_c[half:]]).astype(bf16)
    to_y = jnp.concatenate([total_c[:half], total_b[half:]]).astype(bf16)
    input_grad = total_a + expert_swap(to_x, ACROSS_X).astype(f32) + expert_swap(to_y, ACROSS_Y).astype(f32)
    input_grad = input_grad + expert_swap(total_d, ACROSS_X | ACROSS_Y).astype(f32)
    gate_grad = jnp.sum(jnp.where(named, score_rows.T[:, None, :].astype(f32), 0), axis=2)
    return (input_grad.astype(bf16), gate_grad.astype(bf16), *grads)


def packed_shards(tokens, cotangent, gate_weight, up_weight, down_weight, expert_ids, gates, swap_flags):
    expert_count = lax.axis_size("expert")
    half_axis = expert_count // 2
    my_slot = lax.axis_index("expert")
    row_count, model_width = tokens.shape
    routed = expert_ids.shape[1]
    capacity = row_count * routed * 5 // (4 * expert_count)
    groups = lax.axis_size("dp")
    quarter = model_width // groups
    own_flag = pair_lookup(jnp.reshape(my_slot, (1,)), swap_flags, half_axis)[0]
    flat_ids = expert_ids.reshape(-1)
    weights = (gate_weight, up_weight, down_weight)
    arrived = from_behind((gate_weight, up_weight, down_weight), "expert", half_axis)
    weights = tuple(
        (jnp.where(own_flag == 1, fresh, stay) for fresh, stay in zip(arrived, weights))
    )
    flipped = pair_lookup(flat_ids, swap_flags, half_axis)
    target = jnp.where(flipped == 1, (flat_ids + half_axis) % expert_count, flat_ids)
    copies = row_count * routed
    onehot = (target[:, None] == jnp.arange(expert_count, dtype=jnp.int32)[None, :]).astype(
        jnp.int32
    )
    earlier = jnp.cumsum(onehot, axis=0) - onehot
    position = jnp.sum(earlier * onehot, axis=1)
    buffer_index = target * capacity + position
    source = jnp.zeros((expert_count * capacity,), jnp.int32)
    source = source.at[buffer_index].set(jnp.arange(copies, dtype=jnp.int32) + 1)
    filled = source > 0
    copy_index = jnp.maximum(source - 1, 0)
    token_index = copy_index // routed
    x_buffer = jnp.where(filled[:, None], tokens[token_index], 0)
    dy_buffer = jnp.where(filled[:, None], cotangent[token_index], 0)
    gate_buffer = jnp.where(filled, gates.reshape(-1)[copy_index], 0)
    x_rows, dy_rows, gate_rows = (
        lax.all_to_all(x_buffer, "expert", split_axis=0, concat_axis=0, tiled=True),
        lax.all_to_all(dy_buffer, "expert", split_axis=0, concat_axis=0, tiled=True),
        lax.all_to_all(gate_buffer, "expert", split_axis=0, concat_axis=0, tiled=True),
    )
    w_gate = weights[0][0]
    w_up = weights[1][0]
    w_down = weights[2][0]
    contract_last = (((1,), (1,)), ((), ()))
    pre_gate = lax.dot_general(x_rows, w_gate, contract_last, preferred_element_type=jnp.float32)
    pre_up = lax.dot_general(x_rows, w_up, contract_last, preferred_element_type=jnp.float32)
    sigma = jax.nn.sigmoid(pre_gate)
    active = pre_gate * sigma
    hidden = (active * pre_up).astype(jnp.bfloat16)
    back = lax.dot_general(dy_rows, w_down, contract_last, preferred_element_type=jnp.float32)
    score_part = jnp.sum(hidden.astype(jnp.float32) * back, axis=1)
    grad_hidden = gate_rows.astype(jnp.float32)[:, None] * back
    slope = sigma * (1.0 + pre_gate * (1.0 - sigma))
    grad_gate = (grad_hidden * pre_up * slope).astype(jnp.bfloat16)
    grad_up = (grad_hidden * active).astype(jnp.bfloat16)
    input_part = jnp.dot(grad_gate, w_gate, preferred_element_type=jnp.float32)
    input_part = input_part + jnp.dot(grad_up, w_up, preferred_element_type=jnp.float32)
    scaled = gate_rows[:, None] * dy_rows
    contract_rows = (((0,), (0,)), ((), ()))
    grad_wgate = lax.dot_general(
        grad_gate, x_rows, contract_rows, preferred_element_type=jnp.float32
    )
    grad_wup = lax.dot_general(grad_up, x_rows, contract_rows, preferred_element_type=jnp.float32)
    grad_wdown = lax.dot_general(hidden, scaled, contract_rows, preferred_element_type=jnp.float32)
    scores = lax.psum(score_part, "dp")
    input_share = lax.psum_scatter(input_part, "dp", scatter_dimension=1, tiled=True).astype(
        jnp.bfloat16
    )
    back_rows, back_scores = (
        lax.all_to_all(input_share, "expert", split_axis=0, concat_axis=0, tiled=True),
        lax.all_to_all(
            scores.astype(jnp.bfloat16), "expert", split_axis=0, concat_axis=0, tiled=True
        ),
    )
    per_copy = back_rows[buffer_index].reshape(row_count, routed, quarter)
    input_grad = jnp.sum(per_copy.astype(jnp.float32), axis=1).astype(jnp.bfloat16)
    gate_grad = back_scores[buffer_index].reshape(row_count, routed)
    gradients = (
        grad_wgate.astype(jnp.bfloat16)[None],
        grad_wup.astype(jnp.bfloat16)[None],
        grad_wdown.astype(jnp.bfloat16)[None],
    )
    return (input_grad, gate_grad, gradients[0], gradients[1], gradients[2])


def chosen(tokens, cotangent, gate_weight, up_weight, down_weight, expert_ids, gates, swap_flags):
    capacity = tokens.shape[0] * expert_ids.shape[1] * 5 // (4 * lax.axis_size("expert"))
    body = whole_shards if 2 * capacity >= tokens.shape[0] else packed_shards
    return body(tokens, cotangent, gate_weight, up_weight, down_weight, expert_ids, gates, swap_flags)


def solution(mesh):
    placed = (
        P("expert", None),
        P("expert", None),
        P("expert", "dp", None),
        P("expert", "dp", None),
        P("expert", "dp", None),
        P("expert", None),
        P("expert", None),
        P(),
    )
    return jax.shard_map(
        chosen,
        mesh=mesh,
        in_specs=placed,
        out_specs=(
            P("expert", "dp"),
            P("expert", None),
            P("expert", "dp", None),
            P("expert", "dp", None),
            P("expert", "dp", None),
        ),
        check_vma=False,
    )
```

```python
import functools

import jax
import jax.numpy as jnp
from jax import lax
from jax.experimental import pallas as pl
from jax.experimental.pallas import tpu as pltpu
from jax.sharding import PartitionSpec as P


CONTRACT_LAST = (((1,), (1,)), ((), ()))
CONTRACT_ROWS = (((0,), (0,)), ((), ()))
VMEM = 14 * 1024 * 1024


def from_behind(value, axis, by):
    devices = lax.axis_size(axis)
    return lax.ppermute(value, axis, [(i, (i + by) % devices) for i in range(devices)])


def swap(value, axis, by):
    return lax.ppermute(value, axis, [(i, i ^ by) for i in range(lax.axis_size(axis))])


def pair_lookup(experts, pair_flags, half_axis):
    match = experts[:, None] % half_axis == jnp.arange(half_axis, dtype=jnp.int32)[None, :]
    return jnp.sum(jnp.where(match, pair_flags[None, :], 0), axis=1)


def in_vmem(*values):
    return [pltpu.with_memory_space_constraint(value, pltpu.VMEM) for value in values]


def rows_of(pieces, columns):
    return jnp.concatenate([ref[pl.ds(start, size), columns] for ref, start, size in pieces], axis=0)


def pieces_of(places, refs):
    return [(refs[i], start, size) for i, start, size in places]


def pack_kernel(tokens, cotangent, first, second, sems):
    half = tokens.shape[0] // 2
    copies = []
    for i, (ref, out) in enumerate(((tokens, first), (cotangent, first), (tokens, second), (cotangent, second))):
        copies.append(
            pltpu.make_async_copy(
                ref.at[pl.ds(i // 2 * half, half), :], out.at[pl.ds(i % 2 * half, half), :], sems.at[i]
            )
        )
    for copy in copies:
        copy.start()
    for copy in copies:
        copy.wait()


def pack(tokens, cotangent):
    message = pltpu.VMEM(tokens.shape, tokens.dtype)
    return pl.pallas_call(
        pack_kernel,
        out_shape=(message, message),
        in_specs=[pl.BlockSpec(memory_space=pl.ANY)] * 2,
        out_specs=[pl.BlockSpec(memory_space=pltpu.VMEM)] * 2,
        scratch_shapes=[pltpu.SemaphoreType.DMA((4,))],
        cost_estimate=pl.CostEstimate(flops=1, bytes_accessed=1, transcendentals=0),
        name="pack",
    )(tokens, cotangent)


def activations_kernel(place, x_places, dy_places, count, parts, where_ref, one_ref, two_ref, *refs):
    x_pieces, dy_pieces = pieces_of(x_places, refs), pieces_of(dy_places, refs)
    in_ref, down_ref = refs[count : count + 2]
    acts_ref, score_ref, keep_near, keep_far, give_near, give_far, both = refs[-7:]
    rows, width = keep_near.shape[1], in_ref.shape[1]
    half = rows // 2
    units = down_ref.shape[0]
    chunk = width // parts
    me, group = where_ref[0], where_ref[1]
    first = lax.broadcasted_iota(jnp.int32, (1, rows), 1) < half
    experts = one_ref.shape[0] // 2
    g = jnp.concatenate(
        [
            jnp.where(first, one_ref[pl.ds(me + core, 1), :], two_ref[pl.ds(me + core, 1), :])
            for core in (0, experts)
        ],
        axis=1,
    )
    pre, back = None, None
    for part in range(parts):
        columns = pl.ds(part * chunk, chunk)
        x, dy = rows_of(x_pieces, columns), rows_of(dy_pieces, columns)
        one = lax.dot_general(in_ref[:, columns], x, CONTRACT_LAST, preferred_element_type=jnp.float32)
        two = lax.dot_general(down_ref[:, columns], dy, CONTRACT_LAST, preferred_element_type=jnp.float32)
        pre = one if pre is None else pre + one
        back = two if back is None else back + two
    pre_gate, pre_up = pre[:units], pre[units:]
    sigma = jax.nn.sigmoid(pre_gate)
    active = pre_gate * sigma
    hidden = active * pre_up
    score_ref[...] = jnp.sum(hidden * back, axis=0, keepdims=True)
    grad_hidden = g * back
    slope = sigma * (1.0 + pre_gate * (1.0 - sigma))
    grads = jnp.concatenate([grad_hidden * pre_up * slope, grad_hidden * active], axis=0)
    acts_ref[place, pl.ds(0, 2 * units), :] = grads.astype(jnp.bfloat16)
    acts_ref[place, pl.ds(2 * units, units), :] = (g * hidden).astype(jnp.bfloat16)
    both[...] = grads.T.astype(jnp.bfloat16)
    for part in range(parts):
        columns = pl.ds(pl.multiple_of((group ^ part) * chunk, chunk), chunk)
        share = jnp.dot(both[...], in_ref[:, columns], preferred_element_type=jnp.float32)
        share = share.astype(jnp.bfloat16)
        keep, give = (keep_far, give_far) if part % 2 else (keep_near, give_near)
        keep[part // 2] = share[:rows]
        give[part // 2] = share[rows:]


def activations(place, places, parts, where, tables, held, weights, before):
    operands, x_places, dy_places = held
    width = operands[0].shape[1]
    rows = sum(size for _, _, size in x_places) // 2
    units = weights[1].shape[0]
    bf16 = jnp.bfloat16
    share = pltpu.VMEM((parts // 2, rows, width // parts), bf16)
    return pl.pallas_call(
        functools.partial(activations_kernel, place, x_places, dy_places, len(operands), parts),
        out_shape=(
            pltpu.VMEM((places, 3 * units, 2 * rows), bf16),
            pltpu.VMEM((1, 2 * rows), jnp.float32),
            share,
            share,
            share,
            share,
        ),
        in_specs=[pl.BlockSpec(memory_space=pltpu.SMEM)]
        + [pl.BlockSpec(memory_space=pltpu.VMEM)] * (len(operands) + 4 + len(before)),
        out_specs=[pl.BlockSpec(memory_space=pltpu.VMEM)] * 6,
        scratch_shapes=[pltpu.VMEM((2 * rows, 2 * units), bf16)],
        input_output_aliases={len(operands) + 5: 0} if before else {},
        compiler_params=pltpu.CompilerParams(vmem_limit_bytes=VMEM),
        cost_estimate=pl.CostEstimate(flops=1, bytes_accessed=1, transcendentals=0),
        name="activations",
    )(where, *in_vmem(*tables, *operands, *weights, *before))


def weight_grads_kernel(sources, x_places, dy_places, loaded, parts, flag_ref, *refs):
    count = 1 + max(place[0] for place in x_places + dy_places)
    operands, refs = list(refs[:count]), refs[count:]
    own, other, refs = refs[:2], refs[2:4], refs[4:]
    outs = refs[:3]
    held, acts, results, sems, out_sems = refs[3:]
    units, width = outs[0].shape[1:]
    rows = own[0].shape[2] // 2
    half = rows // 2
    chunk = width // parts
    copies = []
    for part in range(parts):
        columns = pl.ds(part * chunk, chunk)
        copies.append([])
        for i in range(loaded):
            copies[-1].append(
                pltpu.make_async_copy(
                    operands[i].at[:, columns], held.at[i, pl.ds(0, operands[i].shape[0]), columns], sems.at[part, i]
                )
            )
            copies[-1][-1].start()
    for i in range(loaded):
        operands[i] = held.at[i]
    x_pieces, dy_pieces = pieces_of(x_places, operands), pieces_of(dy_places, operands)
    tiles = [(one ^ core, two ^ core) for one, two in sources for core in (0, CORE)]
    first = lax.broadcasted_iota(jnp.int32, (1, rows), 1) < half

    def tile_of(groups_of, place):
        group, early = place // 2, groups_of[0].shape[0]
        ref, group = (groups_of[0], group) if group < early else (groups_of[1], group - early)
        return ref[group, :, pl.ds(place % 2 * rows, rows)]

    for place, (one, two) in enumerate(tiles):
        from_one = [tile[0] for tile in tiles].index(one ^ ACROSS_Y)
        from_two = [tile[1] for tile in tiles].index(two ^ ACROSS_Y)
        arrived = jnp.where(first, tile_of(other, from_one), tile_of(other, from_two))
        acts[:, pl.ds(place * rows, rows)] = jnp.where(flag_ref[0] == 1, arrived, tile_of(own, place))
    sent = []
    for part in range(parts):
        for copy in copies[part]:
            copy.wait()
        columns = pl.ds(part * chunk, chunk)
        x, dy = rows_of(x_pieces, columns), rows_of(dy_pieces, columns)
        both = jnp.dot(acts[pl.ds(0, 2 * units), :], x, preferred_element_type=jnp.float32)
        results[part, pl.ds(0, 2 * units), :] = both.astype(jnp.bfloat16)
        down = jnp.dot(acts[pl.ds(2 * units, units), :], dy, preferred_element_type=jnp.float32)
        results[part, pl.ds(2 * units, units), :] = down.astype(jnp.bfloat16)
        for i, out in enumerate(outs):
            sent.append(
                pltpu.make_async_copy(
                    results.at[part, pl.ds(i * units, units), :], out.at[0, :, columns], out_sems.at[part, i]
                )
            )
            sent[-1].start()
    for copy in sent:
        copy.wait()


def weight_grads(sources, flag, groups, own, other):
    parts, loaded = 4, len(groups[0][0]) + len(groups[1][0])
    operands, x_places, dy_places = [], [], []
    for held, x_of, dy_of in groups:
        x_places += [(i + len(operands), start, size) for i, start, size in x_of]
        dy_places += [(i + len(operands), start, size) for i, start, size in dy_of]
        operands += held
    rows, width = operands[0].shape
    units = own[0].shape[1] // 3
    total = sum(size for _, _, size in x_places)
    bf16 = jnp.bfloat16
    rest = in_vmem(*operands[loaded:], *own, *other)
    return pl.pallas_call(
        functools.partial(weight_grads_kernel, sources, x_places, dy_places, loaded, parts),
        out_shape=(jax.ShapeDtypeStruct((1, units, width), bf16),) * 3,
        in_specs=[pl.BlockSpec(memory_space=pltpu.SMEM)]
        + [pl.BlockSpec(memory_space=pl.ANY)] * loaded
        + [pl.BlockSpec(memory_space=pltpu.VMEM)] * len(rest),
        out_specs=[pl.BlockSpec(memory_space=pl.ANY)] * 3,
        scratch_shapes=[
            pltpu.VMEM((loaded, rows, width), bf16),
            pltpu.VMEM((3 * units, total), bf16),
            pltpu.VMEM((parts, 3 * units, width // parts), bf16),
            pltpu.SemaphoreType.DMA((parts, loaded)),
            pltpu.SemaphoreType.DMA((parts, 3)),
        ],
        compiler_params=pltpu.CompilerParams(vmem_limit_bytes=26 * 1024 * 1024),
        cost_estimate=pl.CostEstimate(flops=1, bytes_accessed=1, transcendentals=0),
        name="weight_grads",
    )(flag, *operands[:loaded], *rest)


CORE, ACROSS_X, ACROSS_Y = 1, 2, 4


def whole_shards(tokens, cotangent, gate_weight, up_weight, down_weight, expert_ids, gates, swap_flags):
    expert_count = lax.axis_size("expert")
    half_axis = expert_count // 2
    me, group = lax.axis_index("expert"), lax.axis_index("dp")
    half = tokens.shape[0] // 2
    parts = lax.axis_size("dp")
    f32, bf16 = jnp.float32, jnp.bfloat16
    own_flag = pair_lookup(jnp.reshape(me, (1,)), swap_flags, half_axis)
    where = jnp.stack([me, group]).astype(jnp.int32)
    weights = (jnp.concatenate([gate_weight[0], up_weight[0]]), down_weight[0])

    def expert_swap(value, by):
        return swap(value, "expert", by)

    def core_swap(message):
        return [expert_swap(message[:half], CORE), expert_swap(message[half:], CORE)]

    rows = 2 * half
    own_block = [tokens, cotangent, expert_swap(tokens, CORE), expert_swap(cotangent, CORE)]
    own_block = (own_block, [(0, 0, rows), (2, 0, rows)], [(1, 0, rows), (3, 0, rows)])
    a, b = {}, {}
    a[0], b[0] = pack(tokens, cotangent)
    a[2], b[4] = expert_swap(a[0], ACROSS_X), expert_swap(b[0], ACROSS_Y)
    a[4], b[2] = expert_swap(a[0], ACROSS_Y), expert_swap(b[0], ACROSS_X)

    named = expert_ids[:, :, None] == jnp.arange(expert_count, dtype=jnp.int32)[None, None, :]
    table = jnp.sum(jnp.where(named, gates[:, :, None].astype(f32), 0), axis=1)
    tables = {0: jnp.concatenate([table.T, expert_swap(table.T, CORE)])}
    tables[2], tables[4] = expert_swap(tables[0], ACROSS_X), expert_swap(tables[0], ACROSS_Y)

    scores, groups = [], []
    barrier = lax.optimization_barrier

    def group_of(one, two):
        mates = core_swap(one) + core_swap(two)
        x_places = [(0, 0, half), (1, 0, half), (2, 0, half), (4, 0, half)]
        dy_places = [(0, half, half), (1, half, half), (3, 0, half), (5, 0, half)]
        return [one, two, *mates], x_places, dy_places

    def work(one, two, held, *before, place=0, places=3):
        acts, score, keep_near, keep_far, give_near, give_far = activations(
            place, places, parts, where, (tables[one], tables[two]), held, weights, before
        )
        scores.append(score)
        groups.append(held)
        return acts, expert_swap(give_far, CORE), (keep_near, keep_far, expert_swap(give_near, CORE))

    def to_neighbour(far, share):
        keep_near, keep_far, near = share
        return keep_near + near, swap(keep_far + far, "dp", 1)

    def to_far(near, arrived):
        near = near + arrived
        return near[0].astype(f32), swap(near[1], "dp", 2)

    acts, far_a, share_a = work(0, 0, own_block)
    a[2], b[4], tables[2], tables[4], acts, far_a = barrier((a[2], b[4], tables[2], tables[4], acts, far_a))
    a[6], b[6] = expert_swap(a[2], ACROSS_Y), expert_swap(b[4], ACROSS_X)
    tables[6] = expert_swap(tables[2], ACROSS_Y)
    near_a, near_in_a = to_neighbour(far_a, share_a)
    acts, far_b, share_b = work(2, 4, group_of(a[2], b[4]), acts, place=1)
    a[4], b[2], tables[6], acts, near_in_a, far_b = barrier((a[4], b[2], tables[6], acts, near_in_a, far_b))
    near_b, near_in_b = to_neighbour(far_b, share_b)
    total_a, far_in_a = to_far(near_a, near_in_a)
    acts, far_c, share_c = work(4, 2, group_of(a[4], b[2]), acts, place=2)
    a[6], b[6], acts, far_in_a, near_in_b, far_c = barrier((a[6], b[6], acts, far_in_a, near_in_b, far_c))
    near_c, near_in_c = to_neighbour(far_c, share_c)
    other = expert_swap(acts, half_axis)
    last_acts, far_d, share_d = work(6, 6, group_of(a[6], b[6]), places=1)
    last_other = expert_swap(last_acts, half_axis)
    total_b, far_in_b = to_far(near_b, near_in_b)
    tiles = jnp.concatenate(scores, axis=1).reshape(expert_count, 2 * half)
    second = jnp.concatenate([tiles[:2, half:], tiles[4:6, half:], tiles[2:4, half:], tiles[6:, half:]])
    score_rows = jnp.concatenate([tiles[:, :half], second], axis=1)
    score_in = swap(score_rows, "dp", 1)
    far_d, score_in, far_in_b, near_in_c, other = barrier((far_d, score_in, far_in_b, near_in_c, other))
    near_d, near_in_d = to_neighbour(far_d, share_d)
    score_rows = score_rows + score_in
    score_rows = score_rows + swap(score_rows, "dp", 2)
    score_rows = jnp.take(score_rows.astype(bf16), jnp.arange(expert_count, dtype=jnp.int32) ^ me, axis=0)
    score_rows = lax.all_to_all(score_rows, "expert", split_axis=0, concat_axis=0, tiled=True)
    total_c, far_in_c = to_far(near_c, near_in_c)
    score_rows, near_in_d, far_in_c, own_flag, last_other = barrier(
        (score_rows, near_in_d, far_in_c, own_flag, last_other)
    )
    total_d, far_in_d = to_far(near_d, near_in_d)
    grads = weight_grads(((0, 0), (2, 4), (4, 2), (6, 6)), own_flag, groups, (acts, last_acts), (other, last_other))
    far_in_d, grads = barrier((far_in_d, grads))

    total_a, total_b = total_a + far_in_a.astype(f32), total_b + far_in_b.astype(f32)
    total_c, total_d = total_c + far_in_c.astype(f32), (total_d + far_in_d.astype(f32)).astype(bf16)
    to_x = jnp.concatenate([total_b[:half], total_c[half:]]).astype(bf16)
    to_y = jnp.concatenate([total_c[:half], total_b[half:]]).astype(bf16)
    input_grad = total_a + expert_swap(to_x, ACROSS_X).astype(f32) + expert_swap(to_y, ACROSS_Y).astype(f32)
    input_grad = input_grad + expert_swap(total_d, ACROSS_X | ACROSS_Y).astype(f32)
    gate_grad = jnp.sum(jnp.where(named, score_rows.T[:, None, :].astype(f32), 0), axis=2)
    return (input_grad.astype(bf16), gate_grad.astype(bf16), *grads)


def packed_shards(tokens, cotangent, gate_weight, up_weight, down_weight, expert_ids, gates, swap_flags):
    expert_count = lax.axis_size("expert")
    half_axis = expert_count // 2
    my_slot = lax.axis_index("expert")
    row_count, model_width = tokens.shape
    routed = expert_ids.shape[1]
    capacity = row_count * routed * 5 // (4 * expert_count)
    groups = lax.axis_size("dp")
    quarter = model_width // groups
    own_flag = pair_lookup(jnp.reshape(my_slot, (1,)), swap_flags, half_axis)[0]
    flat_ids = expert_ids.reshape(-1)
    weights = (gate_weight, up_weight, down_weight)
    arrived = from_behind((gate_weight, up_weight, down_weight), "expert", half_axis)
    weights = tuple(
        (jnp.where(own_flag == 1, fresh, stay) for fresh, stay in zip(arrived, weights))
    )
    flipped = pair_lookup(flat_ids, swap_flags, half_axis)
    target = jnp.where(flipped == 1, (flat_ids + half_axis) % expert_count, flat_ids)
    copies = row_count * routed
    onehot = (target[:, None] == jnp.arange(expert_count, dtype=jnp.int32)[None, :]).astype(
        jnp.int32
    )
    earlier = jnp.cumsum(onehot, axis=0) - onehot
    position = jnp.sum(earlier * onehot, axis=1)
    buffer_index = target * capacity + position
    source = jnp.zeros((expert_count * capacity,), jnp.int32)
    source = source.at[buffer_index].set(jnp.arange(copies, dtype=jnp.int32) + 1)
    filled = source > 0
    copy_index = jnp.maximum(source - 1, 0)
    token_index = copy_index // routed
    x_buffer = jnp.where(filled[:, None], tokens[token_index], 0)
    dy_buffer = jnp.where(filled[:, None], cotangent[token_index], 0)
    gate_buffer = jnp.where(filled, gates.reshape(-1)[copy_index], 0)
    x_rows, dy_rows, gate_rows = (
        lax.all_to_all(x_buffer, "expert", split_axis=0, concat_axis=0, tiled=True),
        lax.all_to_all(dy_buffer, "expert", split_axis=0, concat_axis=0, tiled=True),
        lax.all_to_all(gate_buffer, "expert", split_axis=0, concat_axis=0, tiled=True),
    )
    w_gate = weights[0][0]
    w_up = weights[1][0]
    w_down = weights[2][0]
    contract_last = (((1,), (1,)), ((), ()))
    pre_gate = lax.dot_general(x_rows, w_gate, contract_last, preferred_element_type=jnp.float32)
    pre_up = lax.dot_general(x_rows, w_up, contract_last, preferred_element_type=jnp.float32)
    sigma = jax.nn.sigmoid(pre_gate)
    active = pre_gate * sigma
    hidden = (active * pre_up).astype(jnp.bfloat16)
    back = lax.dot_general(dy_rows, w_down, contract_last, preferred_element_type=jnp.float32)
    score_part = jnp.sum(hidden.astype(jnp.float32) * back, axis=1)
    grad_hidden = gate_rows.astype(jnp.float32)[:, None] * back
    slope = sigma * (1.0 + pre_gate * (1.0 - sigma))
    grad_gate = (grad_hidden * pre_up * slope).astype(jnp.bfloat16)
    grad_up = (grad_hidden * active).astype(jnp.bfloat16)
    input_part = jnp.dot(grad_gate, w_gate, preferred_element_type=jnp.float32)
    input_part = input_part + jnp.dot(grad_up, w_up, preferred_element_type=jnp.float32)
    scaled = gate_rows[:, None] * dy_rows
    contract_rows = (((0,), (0,)), ((), ()))
    grad_wgate = lax.dot_general(
        grad_gate, x_rows, contract_rows, preferred_element_type=jnp.float32
    )
    grad_wup = lax.dot_general(grad_up, x_rows, contract_rows, preferred_element_type=jnp.float32)
    grad_wdown = lax.dot_general(hidden, scaled, contract_rows, preferred_element_type=jnp.float32)
    scores = lax.psum(score_part, "dp")
    input_share = lax.psum_scatter(input_part, "dp", scatter_dimension=1, tiled=True).astype(
        jnp.bfloat16
    )
    back_rows, back_scores = (
        lax.all_to_all(input_share, "expert", split_axis=0, concat_axis=0, tiled=True),
        lax.all_to_all(
            scores.astype(jnp.bfloat16), "expert", split_axis=0, concat_axis=0, tiled=True
        ),
    )
    per_copy = back_rows[buffer_index].reshape(row_count, routed, quarter)
    input_grad = jnp.sum(per_copy.astype(jnp.float32), axis=1).astype(jnp.bfloat16)
    gate_grad = back_scores[buffer_index].reshape(row_count, routed)
    gradients = (
        grad_wgate.astype(jnp.bfloat16)[None],
        grad_wup.astype(jnp.bfloat16)[None],
        grad_wdown.astype(jnp.bfloat16)[None],
    )
    return (input_grad, gate_grad, gradients[0], gradients[1], gradients[2])


def chosen(tokens, cotangent, gate_weight, up_weight, down_weight, expert_ids, gates, swap_flags):
    capacity = tokens.shape[0] * expert_ids.shape[1] * 5 // (4 * lax.axis_size("expert"))
    body = whole_shards if 2 * capacity >= tokens.shape[0] else packed_shards
    return body(tokens, cotangent, gate_weight, up_weight, down_weight, expert_ids, gates, swap_flags)


def solution(mesh):
    placed = (
        P("expert", None),
        P("expert", None),
        P("expert", "dp", None),
        P("expert", "dp", None),
        P("expert", "dp", None),
        P("expert", None),
        P("expert", None),
        P(),
    )
    return jax.shard_map(
        chosen,
        mesh=mesh,
        in_specs=placed,
        out_specs=(
            P("expert", "dp"),
            P("expert", None),
            P("expert", "dp", None),
            P("expert", "dp", None),
            P("expert", "dp", None),
        ),
        check_vma=False,
    )
```

```python
import functools

import jax
import jax.numpy as jnp
from jax import lax
from jax.experimental import pallas as pl
from jax.experimental.pallas import tpu as pltpu
from jax.sharding import PartitionSpec as P


CONTRACT_LAST = (((1,), (1,)), ((), ()))
CONTRACT_ROWS = (((0,), (0,)), ((), ()))
VMEM = 14 * 1024 * 1024


def from_behind(value, axis, by):
    devices = lax.axis_size(axis)
    return lax.ppermute(value, axis, [(i, (i + by) % devices) for i in range(devices)])


def swap(value, axis, by):
    return lax.ppermute(value, axis, [(i, i ^ by) for i in range(lax.axis_size(axis))])


def pair_lookup(experts, pair_flags, half_axis):
    match = experts[:, None] % half_axis == jnp.arange(half_axis, dtype=jnp.int32)[None, :]
    return jnp.sum(jnp.where(match, pair_flags[None, :], 0), axis=1)


def in_vmem(*values):
    return [pltpu.with_memory_space_constraint(value, pltpu.VMEM) for value in values]


def rows_of(pieces, columns):
    return jnp.concatenate([ref[pl.ds(start, size), columns] for ref, start, size in pieces], axis=0)


def pieces_of(places, refs):
    return [(refs[i], start, size) for i, start, size in places]


def pack_kernel(tokens, cotangent, first, second, sems):
    half = tokens.shape[0] // 2
    copies = []
    for i, (ref, out) in enumerate(((tokens, first), (cotangent, first), (tokens, second), (cotangent, second))):
        copies.append(
            pltpu.make_async_copy(
                ref.at[pl.ds(i // 2 * half, half), :], out.at[pl.ds(i % 2 * half, half), :], sems.at[i]
            )
        )
    for copy in copies:
        copy.start()
    for copy in copies:
        copy.wait()


def pack(tokens, cotangent):
    message = pltpu.VMEM(tokens.shape, tokens.dtype)
    return pl.pallas_call(
        pack_kernel,
        out_shape=(message, message),
        in_specs=[pl.BlockSpec(memory_space=pl.ANY)] * 2,
        out_specs=[pl.BlockSpec(memory_space=pltpu.VMEM)] * 2,
        scratch_shapes=[pltpu.SemaphoreType.DMA((4,))],
        cost_estimate=pl.CostEstimate(flops=1, bytes_accessed=1, transcendentals=0),
        name="pack",
    )(tokens, cotangent)


def activations_kernel(place, x_places, dy_places, count, parts, where_ref, one_ref, two_ref, *refs):
    x_pieces, dy_pieces = pieces_of(x_places, refs), pieces_of(dy_places, refs)
    in_ref, down_ref = refs[count : count + 2]
    acts_ref, score_ref, keep_near, keep_far, give_near, give_far, both = refs[-7:]
    rows, width = keep_near.shape[1], in_ref.shape[1]
    half = rows // 2
    units = down_ref.shape[0]
    chunk = width // parts
    me, group = where_ref[0], where_ref[1]
    first = lax.broadcasted_iota(jnp.int32, (1, rows), 1) < half
    experts = one_ref.shape[0] // 2
    g = jnp.concatenate(
        [
            jnp.where(first, one_ref[pl.ds(me + core, 1), :], two_ref[pl.ds(me + core, 1), :])
            for core in (0, experts)
        ],
        axis=1,
    )
    pre, back = None, None
    for part in range(parts):
        columns = pl.ds(part * chunk, chunk)
        x, dy = rows_of(x_pieces, columns), rows_of(dy_pieces, columns)
        one = lax.dot_general(in_ref[:, columns], x, CONTRACT_LAST, preferred_element_type=jnp.float32)
        two = lax.dot_general(down_ref[:, columns], dy, CONTRACT_LAST, preferred_element_type=jnp.float32)
        pre = one if pre is None else pre + one
        back = two if back is None else back + two
    pre_gate, pre_up = pre[:units], pre[units:]
    sigma = jax.nn.sigmoid(pre_gate)
    active = pre_gate * sigma
    hidden = active * pre_up
    score_ref[...] = jnp.sum(hidden * back, axis=0, keepdims=True)
    grad_hidden = g * back
    slope = sigma * (1.0 + pre_gate * (1.0 - sigma))
    grads = jnp.concatenate([grad_hidden * pre_up * slope, grad_hidden * active], axis=0)
    acts_ref[place, pl.ds(0, 2 * units), :] = grads.astype(jnp.bfloat16)
    acts_ref[place, pl.ds(2 * units, units), :] = (g * hidden).astype(jnp.bfloat16)
    both[...] = grads.T.astype(jnp.bfloat16)
    for part in range(parts):
        columns = pl.ds(pl.multiple_of((group ^ part) * chunk, chunk), chunk)
        share = jnp.dot(both[...], in_ref[:, columns], preferred_element_type=jnp.float32)
        share = share.astype(jnp.bfloat16)
        keep, give = (keep_far, give_far) if part % 2 else (keep_near, give_near)
        keep[part // 2] = share[:rows]
        give[part // 2] = share[rows:]


def activations(place, places, parts, where, tables, held, weights, before):
    operands, x_places, dy_places = held
    width = operands[0].shape[1]
    rows = sum(size for _, _, size in x_places) // 2
    units = weights[1].shape[0]
    bf16 = jnp.bfloat16
    share = pltpu.VMEM((parts // 2, rows, width // parts), bf16)
    return pl.pallas_call(
        functools.partial(activations_kernel, place, x_places, dy_places, len(operands), parts),
        out_shape=(
            pltpu.VMEM((places, 3 * units, 2 * rows), bf16),
            pltpu.VMEM((1, 2 * rows), jnp.float32),
            share,
            share,
            share,
            share,
        ),
        in_specs=[pl.BlockSpec(memory_space=pltpu.SMEM)]
        + [pl.BlockSpec(memory_space=pltpu.VMEM)] * (len(operands) + 4 + len(before)),
        out_specs=[pl.BlockSpec(memory_space=pltpu.VMEM)] * 6,
        scratch_shapes=[pltpu.VMEM((2 * rows, 2 * units), bf16)],
        input_output_aliases={len(operands) + 5: 0} if before else {},
        compiler_params=pltpu.CompilerParams(vmem_limit_bytes=VMEM),
        cost_estimate=pl.CostEstimate(flops=1, bytes_accessed=1, transcendentals=0),
        name="activations",
    )(where, *in_vmem(*tables, *operands, *weights, *before))


def weight_grads_kernel(sources, x_places, dy_places, loaded, parts, flag_ref, *refs):
    operands, refs = list(refs[:loaded]), refs[loaded:]
    own, other, refs = refs[:2], refs[2:4], refs[4:]
    outs = refs[:3]
    held, acts, results, sems, out_sems = refs[3:]
    units, width = outs[0].shape[1:]
    rows = own[0].shape[2] // 2
    half = rows // 2
    chunk = width // parts
    copies = []
    for part in range(parts):
        columns = pl.ds(part * chunk, chunk)
        copies.append([])
        for i in range(loaded):
            copies[-1].append(
                pltpu.make_async_copy(operands[i].at[:, columns], held.at[i, :, columns], sems.at[part, i])
            )
            copies[-1][-1].start()
    for i in range(loaded):
        operands[i] = held.at[i]
    x_pieces, dy_pieces = pieces_of(x_places, operands), pieces_of(dy_places, operands)
    tiles = [(one ^ core, two ^ core) for one, two in sources for core in (0, CORE)]
    first = lax.broadcasted_iota(jnp.int32, (1, rows), 1) < half

    def tile_of(groups_of, place):
        group, early = place // 2, groups_of[0].shape[0]
        ref, group = (groups_of[0], group) if group < early else (groups_of[1], group - early)
        return ref[group, :, pl.ds(place % 2 * rows, rows)]

    for place, (one, two) in enumerate(tiles):
        from_one = [tile[0] for tile in tiles].index(one ^ ACROSS_Y)
        from_two = [tile[1] for tile in tiles].index(two ^ ACROSS_Y)
        arrived = jnp.where(first, tile_of(other, from_one), tile_of(other, from_two))
        acts[:, pl.ds(place * rows, rows)] = jnp.where(flag_ref[0] == 1, arrived, tile_of(own, place))
    sent = []
    for part in range(parts):
        for copy in copies[part]:
            copy.wait()
        columns = pl.ds(part * chunk, chunk)
        x, dy = rows_of(x_pieces, columns), rows_of(dy_pieces, columns)
        both = jnp.dot(acts[pl.ds(0, 2 * units), :], x, preferred_element_type=jnp.float32)
        results[part, pl.ds(0, 2 * units), :] = both.astype(jnp.bfloat16)
        down = jnp.dot(acts[pl.ds(2 * units, units), :], dy, preferred_element_type=jnp.float32)
        results[part, pl.ds(2 * units, units), :] = down.astype(jnp.bfloat16)
        for i, out in enumerate(outs):
            sent.append(
                pltpu.make_async_copy(
                    results.at[part, pl.ds(i * units, units), :], out.at[0, :, columns], out_sems.at[part, i]
                )
            )
            sent[-1].start()
    for copy in sent:
        copy.wait()


def weight_grads(sources, flag, groups, own, other):
    parts = 4
    operands, x_places, dy_places = [], [], []
    for held, x_of, dy_of in groups:
        x_places += [(i + len(operands), start, size) for i, start, size in x_of]
        dy_places += [(i + len(operands), start, size) for i, start, size in dy_of]
        operands += held
    rows, width = operands[0].shape
    loaded = len(operands)
    units = own[0].shape[1] // 3
    total = sum(size for _, _, size in x_places)
    bf16 = jnp.bfloat16
    rest = in_vmem(*own, *other)
    return pl.pallas_call(
        functools.partial(weight_grads_kernel, sources, x_places, dy_places, loaded, parts),
        out_shape=(jax.ShapeDtypeStruct((1, units, width), bf16),) * 3,
        in_specs=[pl.BlockSpec(memory_space=pltpu.SMEM)]
        + [pl.BlockSpec(memory_space=pl.ANY)] * loaded
        + [pl.BlockSpec(memory_space=pltpu.VMEM)] * len(rest),
        out_specs=[pl.BlockSpec(memory_space=pl.ANY)] * 3,
        scratch_shapes=[
            pltpu.VMEM((loaded, rows, width), bf16),
            pltpu.VMEM((3 * units, total), bf16),
            pltpu.VMEM((parts, 3 * units, width // parts), bf16),
            pltpu.SemaphoreType.DMA((parts, loaded)),
            pltpu.SemaphoreType.DMA((parts, 3)),
        ],
        compiler_params=pltpu.CompilerParams(vmem_limit_bytes=32 * 1024 * 1024),
        cost_estimate=pl.CostEstimate(flops=1, bytes_accessed=1, transcendentals=0),
        name="weight_grads",
    )(flag, *operands, *rest)


CORE, ACROSS_X, ACROSS_Y = 1, 2, 4


def whole_shards(tokens, cotangent, gate_weight, up_weight, down_weight, expert_ids, gates, swap_flags):
    expert_count = lax.axis_size("expert")
    half_axis = expert_count // 2
    me, group = lax.axis_index("expert"), lax.axis_index("dp")
    half = tokens.shape[0] // 2
    parts = lax.axis_size("dp")
    f32, bf16 = jnp.float32, jnp.bfloat16
    own_flag = pair_lookup(jnp.reshape(me, (1,)), swap_flags, half_axis)
    where = jnp.stack([me, group]).astype(jnp.int32)
    weights = (jnp.concatenate([gate_weight[0], up_weight[0]]), down_weight[0])

    def expert_swap(value, by):
        return swap(value, "expert", by)

    rows = 2 * half
    own_block = [tokens, cotangent, expert_swap(tokens, CORE), expert_swap(cotangent, CORE)]
    own_block = (own_block, [(0, 0, rows), (2, 0, rows)], [(1, 0, rows), (3, 0, rows)])
    a, b = {}, {}
    a[0], b[0] = pack(tokens, cotangent)
    a[2], b[4] = expert_swap(a[0], ACROSS_X), expert_swap(b[0], ACROSS_Y)
    a[4], b[2] = expert_swap(a[0], ACROSS_Y), expert_swap(b[0], ACROSS_X)

    named = expert_ids[:, :, None] == jnp.arange(expert_count, dtype=jnp.int32)[None, None, :]
    table = jnp.sum(jnp.where(named, gates[:, :, None].astype(f32), 0), axis=1)
    tables = {0: jnp.concatenate([table.T, expert_swap(table.T, CORE)])}
    tables[2], tables[4] = expert_swap(tables[0], ACROSS_X), expert_swap(tables[0], ACROSS_Y)

    scores, groups = [], []
    barrier = lax.optimization_barrier

    def group_of(one, two):
        messages = [one, two, expert_swap(one, CORE), expert_swap(two, CORE)]
        return messages, [(i, 0, half) for i in range(4)], [(i, half, half) for i in range(4)]

    def work(one, two, held, *before, place=0, places=3):
        acts, score, keep_near, keep_far, give_near, give_far = activations(
            place, places, parts, where, (tables[one], tables[two]), held, weights, before
        )
        scores.append(score)
        groups.append(held)
        return acts, expert_swap(give_far, CORE), (keep_near, keep_far, expert_swap(give_near, CORE))

    def to_neighbour(far, share):
        keep_near, keep_far, near = share
        return keep_near + near, swap(keep_far + far, "dp", 1)

    def to_far(near, arrived):
        near = near + arrived
        return near[0].astype(f32), swap(near[1], "dp", 2)

    acts, far_a, share_a = work(0, 0, own_block)
    a[2], b[4], tables[2], tables[4], acts, far_a = barrier((a[2], b[4], tables[2], tables[4], acts, far_a))
    a[6], b[6] = expert_swap(a[2], ACROSS_Y), expert_swap(b[4], ACROSS_X)
    tables[6] = expert_swap(tables[2], ACROSS_Y)
    near_a, near_in_a = to_neighbour(far_a, share_a)
    acts, far_b, share_b = work(2, 4, group_of(a[2], b[4]), acts, place=1)
    a[4], b[2], tables[6], acts, near_in_a, far_b = barrier((a[4], b[2], tables[6], acts, near_in_a, far_b))
    near_b, near_in_b = to_neighbour(far_b, share_b)
    total_a, far_in_a = to_far(near_a, near_in_a)
    acts, far_c, share_c = work(4, 2, group_of(a[4], b[2]), acts, place=2)
    a[6], b[6], acts, far_in_a, near_in_b, far_c = barrier((a[6], b[6], acts, far_in_a, near_in_b, far_c))
    near_c, near_in_c = to_neighbour(far_c, share_c)
    other = expert_swap(acts, half_axis)
    last_acts, far_d, share_d = work(6, 6, group_of(a[6], b[6]), places=1)
    last_other = expert_swap(last_acts, half_axis)
    total_b, far_in_b = to_far(near_b, near_in_b)
    tiles = jnp.concatenate(scores, axis=1).reshape(expert_count, 2 * half)
    second = jnp.concatenate([tiles[:2, half:], tiles[4:6, half:], tiles[2:4, half:], tiles[6:, half:]])
    score_rows = jnp.concatenate([tiles[:, :half], second], axis=1)
    score_in = swap(score_rows, "dp", 1)
    far_d, score_in, near_in_c, other = barrier((far_d, score_in, near_in_c, other))
    near_d, near_in_d = to_neighbour(far_d, share_d)
    score_rows = score_rows + score_in
    score_rows = score_rows + swap(score_rows, "dp", 2)
    score_rows = jnp.take(score_rows.astype(bf16), jnp.arange(expert_count, dtype=jnp.int32) ^ me, axis=0)
    score_rows = lax.all_to_all(score_rows, "expert", split_axis=0, concat_axis=0, tiled=True)
    total_c, far_in_c = to_far(near_c, near_in_c)
    grads = weight_grads(
        ((0, 0), (2, 4), (4, 2), (6, 6)), own_flag, groups, (acts, last_acts), (other, last_other)
    )
    score_rows, near_in_d, far_in_b, far_in_c, grads = barrier((score_rows, near_in_d, far_in_b, far_in_c, grads))
    total_d, far_in_d = to_far(near_d, near_in_d)

    total_a, total_b = total_a + far_in_a.astype(f32), total_b + far_in_b.astype(f32)
    total_c, total_d = total_c + far_in_c.astype(f32), (total_d + far_in_d.astype(f32)).astype(bf16)
    to_x = jnp.concatenate([total_b[:half], total_c[half:]]).astype(bf16)
    to_y = jnp.concatenate([total_c[:half], total_b[half:]]).astype(bf16)
    input_grad = total_a + expert_swap(to_x, ACROSS_X).astype(f32) + expert_swap(to_y, ACROSS_Y).astype(f32)
    input_grad = input_grad + expert_swap(total_d, ACROSS_X | ACROSS_Y).astype(f32)
    gate_grad = jnp.sum(jnp.where(named, score_rows.T[:, None, :].astype(f32), 0), axis=2)
    return (input_grad.astype(bf16), gate_grad.astype(bf16), *grads)


def packed_shards(tokens, cotangent, gate_weight, up_weight, down_weight, expert_ids, gates, swap_flags):
    expert_count = lax.axis_size("expert")
    half_axis = expert_count // 2
    my_slot = lax.axis_index("expert")
    row_count, model_width = tokens.shape
    routed = expert_ids.shape[1]
    capacity = row_count * routed * 5 // (4 * expert_count)
    groups = lax.axis_size("dp")
    quarter = model_width // groups
    own_flag = pair_lookup(jnp.reshape(my_slot, (1,)), swap_flags, half_axis)[0]
    flat_ids = expert_ids.reshape(-1)
    weights = (gate_weight, up_weight, down_weight)
    arrived = from_behind((gate_weight, up_weight, down_weight), "expert", half_axis)
    weights = tuple(
        (jnp.where(own_flag == 1, fresh, stay) for fresh, stay in zip(arrived, weights))
    )
    flipped = pair_lookup(flat_ids, swap_flags, half_axis)
    target = jnp.where(flipped == 1, (flat_ids + half_axis) % expert_count, flat_ids)
    copies = row_count * routed
    onehot = (target[:, None] == jnp.arange(expert_count, dtype=jnp.int32)[None, :]).astype(
        jnp.int32
    )
    earlier = jnp.cumsum(onehot, axis=0) - onehot
    position = jnp.sum(earlier * onehot, axis=1)
    buffer_index = target * capacity + position
    source = jnp.zeros((expert_count * capacity,), jnp.int32)
    source = source.at[buffer_index].set(jnp.arange(copies, dtype=jnp.int32) + 1)
    filled = source > 0
    copy_index = jnp.maximum(source - 1, 0)
    token_index = copy_index // routed
    x_buffer = jnp.where(filled[:, None], tokens[token_index], 0)
    dy_buffer = jnp.where(filled[:, None], cotangent[token_index], 0)
    gate_buffer = jnp.where(filled, gates.reshape(-1)[copy_index], 0)
    x_rows, dy_rows, gate_rows = (
        lax.all_to_all(x_buffer, "expert", split_axis=0, concat_axis=0, tiled=True),
        lax.all_to_all(dy_buffer, "expert", split_axis=0, concat_axis=0, tiled=True),
        lax.all_to_all(gate_buffer, "expert", split_axis=0, concat_axis=0, tiled=True),
    )
    w_gate = weights[0][0]
    w_up = weights[1][0]
    w_down = weights[2][0]
    contract_last = (((1,), (1,)), ((), ()))
    pre_gate = lax.dot_general(x_rows, w_gate, contract_last, preferred_element_type=jnp.float32)
    pre_up = lax.dot_general(x_rows, w_up, contract_last, preferred_element_type=jnp.float32)
    sigma = jax.nn.sigmoid(pre_gate)
    active = pre_gate * sigma
    hidden = (active * pre_up).astype(jnp.bfloat16)
    back = lax.dot_general(dy_rows, w_down, contract_last, preferred_element_type=jnp.float32)
    score_part = jnp.sum(hidden.astype(jnp.float32) * back, axis=1)
    grad_hidden = gate_rows.astype(jnp.float32)[:, None] * back
    slope = sigma * (1.0 + pre_gate * (1.0 - sigma))
    grad_gate = (grad_hidden * pre_up * slope).astype(jnp.bfloat16)
    grad_up = (grad_hidden * active).astype(jnp.bfloat16)
    input_part = jnp.dot(grad_gate, w_gate, preferred_element_type=jnp.float32)
    input_part = input_part + jnp.dot(grad_up, w_up, preferred_element_type=jnp.float32)
    scaled = gate_rows[:, None] * dy_rows
    contract_rows = (((0,), (0,)), ((), ()))
    grad_wgate = lax.dot_general(
        grad_gate, x_rows, contract_rows, preferred_element_type=jnp.float32
    )
    grad_wup = lax.dot_general(grad_up, x_rows, contract_rows, preferred_element_type=jnp.float32)
    grad_wdown = lax.dot_general(hidden, scaled, contract_rows, preferred_element_type=jnp.float32)
    scores = lax.psum(score_part, "dp")
    input_share = lax.psum_scatter(input_part, "dp", scatter_dimension=1, tiled=True).astype(
        jnp.bfloat16
    )
    back_rows, back_scores = (
        lax.all_to_all(input_share, "expert", split_axis=0, concat_axis=0, tiled=True),
        lax.all_to_all(
            scores.astype(jnp.bfloat16), "expert", split_axis=0, concat_axis=0, tiled=True
        ),
    )
    per_copy = back_rows[buffer_index].reshape(row_count, routed, quarter)
    input_grad = jnp.sum(per_copy.astype(jnp.float32), axis=1).astype(jnp.bfloat16)
    gate_grad = back_scores[buffer_index].reshape(row_count, routed)
    gradients = (
        grad_wgate.astype(jnp.bfloat16)[None],
        grad_wup.astype(jnp.bfloat16)[None],
        grad_wdown.astype(jnp.bfloat16)[None],
    )
    return (input_grad, gate_grad, gradients[0], gradients[1], gradients[2])


def chosen(tokens, cotangent, gate_weight, up_weight, down_weight, expert_ids, gates, swap_flags):
    capacity = tokens.shape[0] * expert_ids.shape[1] * 5 // (4 * lax.axis_size("expert"))
    body = whole_shards if 2 * capacity >= tokens.shape[0] else packed_shards
    return body(tokens, cotangent, gate_weight, up_weight, down_weight, expert_ids, gates, swap_flags)


def solution(mesh):
    placed = (
        P("expert", None),
        P("expert", None),
        P("expert", "dp", None),
        P("expert", "dp", None),
        P("expert", "dp", None),
        P("expert", None),
        P("expert", None),
        P(),
    )
    return jax.shard_map(
        chosen,
        mesh=mesh,
        in_specs=placed,
        out_specs=(
            P("expert", "dp"),
            P("expert", None),
            P("expert", "dp", None),
            P("expert", "dp", None),
            P("expert", "dp", None),
        ),
        check_vma=False,
    )
```

```python
import functools

import jax
import jax.numpy as jnp
from jax import lax
from jax.experimental import pallas as pl
from jax.experimental.pallas import tpu as pltpu
from jax.sharding import PartitionSpec as P


CONTRACT_LAST = (((1,), (1,)), ((), ()))
CONTRACT_ROWS = (((0,), (0,)), ((), ()))
VMEM = 14 * 1024 * 1024


def from_behind(value, axis, by):
    devices = lax.axis_size(axis)
    return lax.ppermute(value, axis, [(i, (i + by) % devices) for i in range(devices)])


def swap(value, axis, by):
    return lax.ppermute(value, axis, [(i, i ^ by) for i in range(lax.axis_size(axis))])


def pair_lookup(experts, pair_flags, half_axis):
    match = experts[:, None] % half_axis == jnp.arange(half_axis, dtype=jnp.int32)[None, :]
    return jnp.sum(jnp.where(match, pair_flags[None, :], 0), axis=1)


def in_vmem(*values):
    return [pltpu.with_memory_space_constraint(value, pltpu.VMEM) for value in values]


def rows_of(pieces, columns):
    return jnp.concatenate([ref[pl.ds(start, size), columns] for ref, start, size in pieces], axis=0)


def pieces_of(places, refs):
    return [(refs[i], start, size) for i, start, size in places]


def pack_kernel(tokens, cotangent, first, second, sems):
    half = tokens.shape[0] // 2
    copies = []
    for i, (ref, out) in enumerate(((tokens, first), (cotangent, first), (tokens, second), (cotangent, second))):
        copies.append(
            pltpu.make_async_copy(
                ref.at[pl.ds(i // 2 * half, half), :], out.at[pl.ds(i % 2 * half, half), :], sems.at[i]
            )
        )
    for copy in copies:
        copy.start()
    for copy in copies:
        copy.wait()


def pack(tokens, cotangent):
    message = pltpu.VMEM(tokens.shape, tokens.dtype)
    return pl.pallas_call(
        pack_kernel,
        out_shape=(message, message),
        in_specs=[pl.BlockSpec(memory_space=pl.ANY)] * 2,
        out_specs=[pl.BlockSpec(memory_space=pltpu.VMEM)] * 2,
        scratch_shapes=[pltpu.SemaphoreType.DMA((4,))],
        compiler_params=pltpu.CompilerParams(vmem_limit_bytes=4 * 1024 * 1024),
        cost_estimate=pl.CostEstimate(flops=1, bytes_accessed=1, transcendentals=0),
        name="pack",
    )(tokens, cotangent)


def activations_kernel(x_places, dy_places, count, parts, where_ref, one_ref, two_ref, *refs):
    x_pieces, dy_pieces = pieces_of(x_places, refs), pieces_of(dy_places, refs)
    in_ref, down_ref = refs[count : count + 2]
    acts_ref, score_ref, keep_near, keep_far, give_near, give_far, both = refs[-7:]
    rows, width = keep_near.shape[1], in_ref.shape[1]
    half = rows // 2
    units = down_ref.shape[0]
    chunk = width // parts
    me, group = where_ref[0], where_ref[1]
    first = lax.broadcasted_iota(jnp.int32, (1, rows), 1) < half
    experts = one_ref.shape[0] // 2
    g = jnp.concatenate(
        [
            jnp.where(first, one_ref[pl.ds(me + core, 1), :], two_ref[pl.ds(me + core, 1), :])
            for core in (0, experts)
        ],
        axis=1,
    )
    pre, back = None, None
    for part in range(parts):
        columns = pl.ds(part * chunk, chunk)
        x, dy = rows_of(x_pieces, columns), rows_of(dy_pieces, columns)
        one = lax.dot_general(in_ref[:, columns], x, CONTRACT_LAST, preferred_element_type=jnp.float32)
        two = lax.dot_general(down_ref[:, columns], dy, CONTRACT_LAST, preferred_element_type=jnp.float32)
        pre = one if pre is None else pre + one
        back = two if back is None else back + two
    pre_gate, pre_up = pre[:units], pre[units:]
    sigma = jax.nn.sigmoid(pre_gate)
    active = pre_gate * sigma
    hidden = active * pre_up
    score_ref[...] = jnp.sum(hidden * back, axis=0, keepdims=True)
    grad_hidden = g * back
    slope = sigma * (1.0 + pre_gate * (1.0 - sigma))
    grads = jnp.concatenate([grad_hidden * pre_up * slope, grad_hidden * active], axis=0)
    acts_ref[pl.ds(0, 2 * units), :] = grads.astype(jnp.bfloat16)
    acts_ref[pl.ds(2 * units, units), :] = (g * hidden).astype(jnp.bfloat16)
    both[...] = grads.T.astype(jnp.bfloat16)
    for part in range(parts):
        columns = pl.ds(pl.multiple_of((group ^ part) * chunk, chunk), chunk)
        share = jnp.dot(both[...], in_ref[:, columns], preferred_element_type=jnp.float32)
        share = share.astype(jnp.bfloat16)
        keep, give = (keep_far, give_far) if part % 2 else (keep_near, give_near)
        keep[part // 2] = share[:rows]
        give[part // 2] = share[rows:]


def activations(parts, where, tables, held, weights):
    operands, x_places, dy_places = held
    width = operands[0].shape[1]
    rows = sum(size for _, _, size in x_places) // 2
    units = weights[1].shape[0]
    bf16 = jnp.bfloat16
    share = pltpu.VMEM((parts // 2, rows, width // parts), bf16)
    return pl.pallas_call(
        functools.partial(activations_kernel, x_places, dy_places, len(operands), parts),
        out_shape=(
            pltpu.VMEM((3 * units, 2 * rows), bf16),
            pltpu.VMEM((1, 2 * rows), jnp.float32),
            share,
            share,
            share,
            share,
        ),
        in_specs=[pl.BlockSpec(memory_space=pltpu.SMEM)]
        + [pl.BlockSpec(memory_space=pltpu.VMEM)] * (len(operands) + 4),
        out_specs=[pl.BlockSpec(memory_space=pltpu.VMEM)] * 6,
        scratch_shapes=[pltpu.VMEM((2 * rows, 2 * units), bf16)],
        compiler_params=pltpu.CompilerParams(vmem_limit_bytes=VMEM),
        cost_estimate=pl.CostEstimate(flops=1, bytes_accessed=1, transcendentals=0),
        name="activations",
    )(where, *in_vmem(*tables, *operands, *weights))


def weight_grads_kernel(sources, x_places, dy_places, loaded, parts, flag_ref, *refs):
    operands, refs = list(refs[:loaded]), refs[loaded:]
    count = len(sources)
    own, other, refs = refs[:count], refs[count : 2 * count], refs[2 * count :]
    outs = refs[:3]
    held, acts, results, sems, out_sems = refs[3:]
    units, width = outs[0].shape[1:]
    rows = own[0].shape[1] // 2
    half = rows // 2
    chunk = width // parts
    copies = []
    for part in range(parts):
        columns = pl.ds(part * chunk, chunk)
        copies.append([])
        for i in range(loaded):
            copies[-1].append(
                pltpu.make_async_copy(operands[i].at[:, columns], held.at[i, :, columns], sems.at[part, i])
            )
            copies[-1][-1].start()
    for i in range(loaded):
        operands[i] = held.at[i]
    x_pieces, dy_pieces = pieces_of(x_places, operands), pieces_of(dy_places, operands)
    tiles = [(one ^ core, two ^ core) for one, two in sources for core in (0, CORE)]
    first = lax.broadcasted_iota(jnp.int32, (1, rows), 1) < half

    def tile_of(groups_of, place):
        return groups_of[place // 2][:, pl.ds(place % 2 * rows, rows)]

    for place, (one, two) in enumerate(tiles):
        from_one = [tile[0] for tile in tiles].index(one ^ ACROSS_Y)
        from_two = [tile[1] for tile in tiles].index(two ^ ACROSS_Y)
        arrived = jnp.where(first, tile_of(other, from_one), tile_of(other, from_two))
        acts[:, pl.ds(place * rows, rows)] = jnp.where(flag_ref[0] == 1, arrived, tile_of(own, place))
    sent = []
    for part in range(parts):
        for copy in copies[part]:
            copy.wait()
        columns = pl.ds(part * chunk, chunk)
        x, dy = rows_of(x_pieces, columns), rows_of(dy_pieces, columns)
        both = jnp.dot(acts[pl.ds(0, 2 * units), :], x, preferred_element_type=jnp.float32)
        results[part, pl.ds(0, 2 * units), :] = both.astype(jnp.bfloat16)
        down = jnp.dot(acts[pl.ds(2 * units, units), :], dy, preferred_element_type=jnp.float32)
        results[part, pl.ds(2 * units, units), :] = down.astype(jnp.bfloat16)
        for i, out in enumerate(outs):
            sent.append(
                pltpu.make_async_copy(
                    results.at[part, pl.ds(i * units, units), :], out.at[0, :, columns], out_sems.at[part, i]
                )
            )
            sent[-1].start()
    for copy in sent:
        copy.wait()


def weight_grads(sources, flag, groups, own, other):
    parts = 4
    operands, x_places, dy_places = [], [], []
    for held, x_of, dy_of in groups:
        x_places += [(i + len(operands), start, size) for i, start, size in x_of]
        dy_places += [(i + len(operands), start, size) for i, start, size in dy_of]
        operands += held
    rows, width = operands[0].shape
    loaded = len(operands)
    units = own[0].shape[0] // 3
    total = sum(size for _, _, size in x_places)
    bf16 = jnp.bfloat16
    rest = in_vmem(*own, *other)
    return pl.pallas_call(
        functools.partial(weight_grads_kernel, sources, x_places, dy_places, loaded, parts),
        out_shape=(jax.ShapeDtypeStruct((1, units, width), bf16),) * 3,
        in_specs=[pl.BlockSpec(memory_space=pltpu.SMEM)]
        + [pl.BlockSpec(memory_space=pl.ANY)] * loaded
        + [pl.BlockSpec(memory_space=pltpu.VMEM)] * len(rest),
        out_specs=[pl.BlockSpec(memory_space=pl.ANY)] * 3,
        scratch_shapes=[
            pltpu.VMEM((loaded, rows, width), bf16),
            pltpu.VMEM((3 * units, total), bf16),
            pltpu.VMEM((parts, 3 * units, width // parts), bf16),
            pltpu.SemaphoreType.DMA((parts, loaded)),
            pltpu.SemaphoreType.DMA((parts, 3)),
        ],
        compiler_params=pltpu.CompilerParams(vmem_limit_bytes=28 * 1024 * 1024),
        cost_estimate=pl.CostEstimate(flops=1, bytes_accessed=1, transcendentals=0),
        name="weight_grads",
    )(flag, *[pltpu.with_memory_space_constraint(value, pltpu.HBM) for value in operands], *rest)


CORE, ACROSS_X, ACROSS_Y = 1, 2, 4


def whole_shards(tokens, cotangent, gate_weight, up_weight, down_weight, expert_ids, gates, swap_flags):
    expert_count = lax.axis_size("expert")
    half_axis = expert_count // 2
    me, group = lax.axis_index("expert"), lax.axis_index("dp")
    half = tokens.shape[0] // 2
    parts = lax.axis_size("dp")
    f32, bf16 = jnp.float32, jnp.bfloat16
    own_flag = pair_lookup(jnp.reshape(me, (1,)), swap_flags, half_axis)
    where = jnp.stack([me, group]).astype(jnp.int32)
    weights = (jnp.concatenate([gate_weight[0], up_weight[0]]), down_weight[0])

    def expert_swap(value, by):
        return swap(value, "expert", by)

    rows = 2 * half
    own_block = [tokens, cotangent, expert_swap(tokens, CORE), expert_swap(cotangent, CORE)]
    own_block = (own_block, [(0, 0, rows), (2, 0, rows)], [(1, 0, rows), (3, 0, rows)])
    a, b = {}, {}
    a[0], b[0] = pack(tokens, cotangent)
    a[2], b[4] = expert_swap(a[0], ACROSS_X), expert_swap(b[0], ACROSS_Y)
    a[4], b[2] = expert_swap(a[0], ACROSS_Y), expert_swap(b[0], ACROSS_X)

    named = expert_ids[:, :, None] == jnp.arange(expert_count, dtype=jnp.int32)[None, None, :]
    table = jnp.sum(jnp.where(named, gates[:, :, None].astype(f32), 0), axis=1)
    tables = {0: jnp.concatenate([table.T, expert_swap(table.T, CORE)])}
    tables[2], tables[4] = expert_swap(tables[0], ACROSS_X), expert_swap(tables[0], ACROSS_Y)

    scores, groups = [], []
    barrier = lax.optimization_barrier

    def group_of(one, two):
        messages = [one, two, expert_swap(one, CORE), expert_swap(two, CORE)]
        return messages, [(i, 0, half) for i in range(4)], [(i, half, half) for i in range(4)]

    def work(one, two, held):
        acts, score, keep_near, keep_far, give_near, give_far = activations(
            parts, where, (tables[one], tables[two]), held, weights
        )
        scores.append(score)
        groups.append(held)
        return acts, expert_swap(give_far, CORE), (keep_near, keep_far, expert_swap(give_near, CORE))

    def to_neighbour(far, share):
        keep_near, keep_far, near = share
        return keep_near + near, swap(keep_far + far, "dp", 1)

    def to_far(near, arrived):
        near = near + arrived
        return near[0].astype(f32), swap(near[1], "dp", 2)

    acts_a, far_a, share_a = work(0, 0, own_block)
    a[2], b[4], tables[2], tables[4], acts_a, far_a = barrier((a[2], b[4], tables[2], tables[4], acts_a, far_a))
    a[6], b[6] = expert_swap(a[2], ACROSS_Y), expert_swap(b[4], ACROSS_X)
    tables[6] = expert_swap(tables[2], ACROSS_Y)
    near_a, near_in_a = to_neighbour(far_a, share_a)
    acts_b, far_b, share_b = work(2, 4, group_of(a[2], b[4]))
    a[4], b[2], tables[6], acts_b, near_in_a, far_b = barrier((a[4], b[2], tables[6], acts_b, near_in_a, far_b))
    near_b, near_in_b = to_neighbour(far_b, share_b)
    total_a, far_in_a = to_far(near_a, near_in_a)
    acts_c, far_c, share_c = work(4, 2, group_of(a[4], b[2]))
    a[6], b[6], acts_c, far_in_a, near_in_b, far_c = barrier((a[6], b[6], acts_c, far_in_a, near_in_b, far_c))
    near_c, near_in_c = to_neighbour(far_c, share_c)
    other_a, other_b = expert_swap(acts_a, half_axis), expert_swap(acts_b, half_axis)
    acts_d, far_d, share_d = work(6, 6, group_of(a[6], b[6]))
    other_c, other_d = expert_swap(acts_c, half_axis), expert_swap(acts_d, half_axis)
    total_b, far_in_b = to_far(near_b, near_in_b)
    tiles = jnp.concatenate(scores, axis=1).reshape(expert_count, 2 * half)
    second = jnp.concatenate([tiles[:2, half:], tiles[4:6, half:], tiles[2:4, half:], tiles[6:, half:]])
    score_rows = jnp.concatenate([tiles[:, :half], second], axis=1)
    score_in = swap(score_rows, "dp", 1)
    far_d, score_in, near_in_c, other_a, other_b = barrier((far_d, score_in, near_in_c, other_a, other_b))
    near_d, near_in_d = to_neighbour(far_d, share_d)
    score_rows = score_rows + score_in
    score_rows = score_rows + swap(score_rows, "dp", 2)
    score_rows = jnp.take(score_rows.astype(bf16), jnp.arange(expert_count, dtype=jnp.int32) ^ me, axis=0)
    score_rows = lax.all_to_all(score_rows, "expert", split_axis=0, concat_axis=0, tiled=True)
    total_c, far_in_c = to_far(near_c, near_in_c)
    score_rows, near_in_d, far_in_b, far_in_c, other_c, other_d, own_flag = barrier(
        (score_rows, near_in_d, far_in_b, far_in_c, other_c, other_d, own_flag)
    )
    total_d, far_in_d = to_far(near_d, near_in_d)
    own, other = (acts_a, acts_b, acts_c, acts_d), (other_a, other_b, other_c, other_d)
    grads = weight_grads(((0, 0), (2, 4), (4, 2), (6, 6)), own_flag, groups, own, other)
    far_in_d, grads = barrier((far_in_d, grads))

    total_a, total_b = total_a + far_in_a.astype(f32), total_b + far_in_b.astype(f32)
    total_c, total_d = total_c + far_in_c.astype(f32), (total_d + far_in_d.astype(f32)).astype(bf16)
    to_x = jnp.concatenate([total_b[:half], total_c[half:]]).astype(bf16)
    to_y = jnp.concatenate([total_c[:half], total_b[half:]]).astype(bf16)
    input_grad = total_a + expert_swap(to_x, ACROSS_X).astype(f32) + expert_swap(to_y, ACROSS_Y).astype(f32)
    input_grad = input_grad + expert_swap(total_d, ACROSS_X | ACROSS_Y).astype(f32)
    gate_grad = jnp.sum(jnp.where(named, score_rows.T[:, None, :].astype(f32), 0), axis=2)
    return (input_grad.astype(bf16), gate_grad.astype(bf16), *grads)


def packed_shards(tokens, cotangent, gate_weight, up_weight, down_weight, expert_ids, gates, swap_flags):
    expert_count = lax.axis_size("expert")
    half_axis = expert_count // 2
    my_slot = lax.axis_index("expert")
    row_count, model_width = tokens.shape
    routed = expert_ids.shape[1]
    capacity = row_count * routed * 5 // (4 * expert_count)
    groups = lax.axis_size("dp")
    quarter = model_width // groups
    own_flag = pair_lookup(jnp.reshape(my_slot, (1,)), swap_flags, half_axis)[0]
    flat_ids = expert_ids.reshape(-1)
    weights = (gate_weight, up_weight, down_weight)
    arrived = from_behind((gate_weight, up_weight, down_weight), "expert", half_axis)
    weights = tuple(
        (jnp.where(own_flag == 1, fresh, stay) for fresh, stay in zip(arrived, weights))
    )
    flipped = pair_lookup(flat_ids, swap_flags, half_axis)
    target = jnp.where(flipped == 1, (flat_ids + half_axis) % expert_count, flat_ids)
    copies = row_count * routed
    onehot = (target[:, None] == jnp.arange(expert_count, dtype=jnp.int32)[None, :]).astype(
        jnp.int32
    )
    earlier = jnp.cumsum(onehot, axis=0) - onehot
    position = jnp.sum(earlier * onehot, axis=1)
    buffer_index = target * capacity + position
    source = jnp.zeros((expert_count * capacity,), jnp.int32)
    source = source.at[buffer_index].set(jnp.arange(copies, dtype=jnp.int32) + 1)
    filled = source > 0
    copy_index = jnp.maximum(source - 1, 0)
    token_index = copy_index // routed
    x_buffer = jnp.where(filled[:, None], tokens[token_index], 0)
    dy_buffer = jnp.where(filled[:, None], cotangent[token_index], 0)
    gate_buffer = jnp.where(filled, gates.reshape(-1)[copy_index], 0)
    x_rows, dy_rows, gate_rows = (
        lax.all_to_all(x_buffer, "expert", split_axis=0, concat_axis=0, tiled=True),
        lax.all_to_all(dy_buffer, "expert", split_axis=0, concat_axis=0, tiled=True),
        lax.all_to_all(gate_buffer, "expert", split_axis=0, concat_axis=0, tiled=True),
    )
    w_gate = weights[0][0]
    w_up = weights[1][0]
    w_down = weights[2][0]
    contract_last = (((1,), (1,)), ((), ()))
    pre_gate = lax.dot_general(x_rows, w_gate, contract_last, preferred_element_type=jnp.float32)
    pre_up = lax.dot_general(x_rows, w_up, contract_last, preferred_element_type=jnp.float32)
    sigma = jax.nn.sigmoid(pre_gate)
    active = pre_gate * sigma
    hidden = (active * pre_up).astype(jnp.bfloat16)
    back = lax.dot_general(dy_rows, w_down, contract_last, preferred_element_type=jnp.float32)
    score_part = jnp.sum(hidden.astype(jnp.float32) * back, axis=1)
    grad_hidden = gate_rows.astype(jnp.float32)[:, None] * back
    slope = sigma * (1.0 + pre_gate * (1.0 - sigma))
    grad_gate = (grad_hidden * pre_up * slope).astype(jnp.bfloat16)
    grad_up = (grad_hidden * active).astype(jnp.bfloat16)
    input_part = jnp.dot(grad_gate, w_gate, preferred_element_type=jnp.float32)
    input_part = input_part + jnp.dot(grad_up, w_up, preferred_element_type=jnp.float32)
    scaled = gate_rows[:, None] * dy_rows
    contract_rows = (((0,), (0,)), ((), ()))
    grad_wgate = lax.dot_general(
        grad_gate, x_rows, contract_rows, preferred_element_type=jnp.float32
    )
    grad_wup = lax.dot_general(grad_up, x_rows, contract_rows, preferred_element_type=jnp.float32)
    grad_wdown = lax.dot_general(hidden, scaled, contract_rows, preferred_element_type=jnp.float32)
    scores = lax.psum(score_part, "dp")
    input_share = lax.psum_scatter(input_part, "dp", scatter_dimension=1, tiled=True).astype(
        jnp.bfloat16
    )
    back_rows, back_scores = (
        lax.all_to_all(input_share, "expert", split_axis=0, concat_axis=0, tiled=True),
        lax.all_to_all(
            scores.astype(jnp.bfloat16), "expert", split_axis=0, concat_axis=0, tiled=True
        ),
    )
    per_copy = back_rows[buffer_index].reshape(row_count, routed, quarter)
    input_grad = jnp.sum(per_copy.astype(jnp.float32), axis=1).astype(jnp.bfloat16)
    gate_grad = back_scores[buffer_index].reshape(row_count, routed)
    gradients = (
        grad_wgate.astype(jnp.bfloat16)[None],
        grad_wup.astype(jnp.bfloat16)[None],
        grad_wdown.astype(jnp.bfloat16)[None],
    )
    return (input_grad, gate_grad, gradients[0], gradients[1], gradients[2])


def chosen(tokens, cotangent, gate_weight, up_weight, down_weight, expert_ids, gates, swap_flags):
    capacity = tokens.shape[0] * expert_ids.shape[1] * 5 // (4 * lax.axis_size("expert"))
    body = whole_shards if 2 * capacity >= tokens.shape[0] else packed_shards
    return body(tokens, cotangent, gate_weight, up_weight, down_weight, expert_ids, gates, swap_flags)


def solution(mesh):
    placed = (
        P("expert", None),
        P("expert", None),
        P("expert", "dp", None),
        P("expert", "dp", None),
        P("expert", "dp", None),
        P("expert", None),
        P("expert", None),
        P(),
    )
    return jax.shard_map(
        chosen,
        mesh=mesh,
        in_specs=placed,
        out_specs=(
            P("expert", "dp"),
            P("expert", None),
            P("expert", "dp", None),
            P("expert", "dp", None),
            P("expert", "dp", None),
        ),
        check_vma=False,
    )
```

```python
import functools

import jax
import jax.numpy as jnp
from jax import lax
from jax.experimental import pallas as pl
from jax.experimental.pallas import tpu as pltpu
from jax.sharding import PartitionSpec as P


CONTRACT_LAST = (((1,), (1,)), ((), ()))
CONTRACT_ROWS = (((0,), (0,)), ((), ()))
VMEM = 14 * 1024 * 1024


def from_behind(value, axis, by):
    devices = lax.axis_size(axis)
    return lax.ppermute(value, axis, [(i, (i + by) % devices) for i in range(devices)])


def swap(value, axis, by):
    return lax.ppermute(value, axis, [(i, i ^ by) for i in range(lax.axis_size(axis))])


def pair_lookup(experts, pair_flags, half_axis):
    match = experts[:, None] % half_axis == jnp.arange(half_axis, dtype=jnp.int32)[None, :]
    return jnp.sum(jnp.where(match, pair_flags[None, :], 0), axis=1)


def in_vmem(*values):
    return [pltpu.with_memory_space_constraint(value, pltpu.VMEM) for value in values]


def rows_of(pieces, columns):
    return jnp.concatenate([ref[pl.ds(start, size), columns] for ref, start, size in pieces], axis=0)


def pieces_of(places, refs):
    return [(refs[i], start, size) for i, start, size in places]


def pack_kernel(tokens, cotangent, first, second, sems):
    half = tokens.shape[0] // 2
    copies = []
    for i, (ref, out) in enumerate(((tokens, first), (cotangent, first), (tokens, second), (cotangent, second))):
        copies.append(
            pltpu.make_async_copy(
                ref.at[pl.ds(i // 2 * half, half), :], out.at[pl.ds(i % 2 * half, half), :], sems.at[i]
            )
        )
    for copy in copies:
        copy.start()
    for copy in copies:
        copy.wait()


def pack(tokens, cotangent):
    message = pltpu.VMEM(tokens.shape, tokens.dtype)
    return pl.pallas_call(
        pack_kernel,
        out_shape=(message, message),
        in_specs=[pl.BlockSpec(memory_space=pl.ANY)] * 2,
        out_specs=[pl.BlockSpec(memory_space=pltpu.VMEM)] * 2,
        scratch_shapes=[pltpu.SemaphoreType.DMA((4,))],
        compiler_params=pltpu.CompilerParams(vmem_limit_bytes=4 * 1024 * 1024),
        cost_estimate=pl.CostEstimate(flops=1, bytes_accessed=1, transcendentals=0),
        name="pack",
    )(*[pltpu.with_memory_space_constraint(value, pltpu.HBM) for value in (tokens, cotangent)])


def activations_kernel(x_places, dy_places, count, parts, where_ref, one_ref, two_ref, *refs):
    x_pieces, dy_pieces = pieces_of(x_places, refs), pieces_of(dy_places, refs)
    in_ref, down_ref = refs[count : count + 2]
    acts_ref, score_ref, keep_near, keep_far, give_near, give_far, both = refs[-7:]
    rows, width = keep_near.shape[1], in_ref.shape[1]
    half = rows // 2
    units = down_ref.shape[0]
    chunk = width // parts
    me, group = where_ref[0], where_ref[1]
    first = lax.broadcasted_iota(jnp.int32, (1, rows), 1) < half
    experts = one_ref.shape[0] // 2
    g = jnp.concatenate(
        [
            jnp.where(first, one_ref[pl.ds(me + core, 1), :], two_ref[pl.ds(me + core, 1), :])
            for core in (0, experts)
        ],
        axis=1,
    )
    pre, back = None, None
    for part in range(parts):
        columns = pl.ds(part * chunk, chunk)
        x, dy = rows_of(x_pieces, columns), rows_of(dy_pieces, columns)
        one = lax.dot_general(in_ref[:, columns], x, CONTRACT_LAST, preferred_element_type=jnp.float32)
        two = lax.dot_general(down_ref[:, columns], dy, CONTRACT_LAST, preferred_element_type=jnp.float32)
        pre = one if pre is None else pre + one
        back = two if back is None else back + two
    pre_gate, pre_up = pre[:units], pre[units:]
    sigma = jax.nn.sigmoid(pre_gate)
    active = pre_gate * sigma
    hidden = active * pre_up
    score_ref[...] = jnp.sum(hidden * back, axis=0, keepdims=True)
    grad_hidden = g * back
    slope = sigma * (1.0 + pre_gate * (1.0 - sigma))
    grads = jnp.concatenate([grad_hidden * pre_up * slope, grad_hidden * active], axis=0)
    acts_ref[pl.ds(0, 2 * units), :] = grads.astype(jnp.bfloat16)
    acts_ref[pl.ds(2 * units, units), :] = (g * hidden).astype(jnp.bfloat16)
    both[...] = grads.T.astype(jnp.bfloat16)
    for part in range(parts):
        columns = pl.ds(pl.multiple_of((group ^ part) * chunk, chunk), chunk)
        share = jnp.dot(both[...], in_ref[:, columns], preferred_element_type=jnp.float32)
        share = share.astype(jnp.bfloat16)
        keep, give = (keep_far, give_far) if part % 2 else (keep_near, give_near)
        keep[part // 2] = share[:rows]
        give[part // 2] = share[rows:]


def activations(parts, where, tables, held, weights):
    operands, x_places, dy_places = held
    width = operands[0].shape[1]
    rows = sum(size for _, _, size in x_places) // 2
    units = weights[1].shape[0]
    bf16 = jnp.bfloat16
    share = pltpu.VMEM((parts // 2, rows, width // parts), bf16)
    return pl.pallas_call(
        functools.partial(activations_kernel, x_places, dy_places, len(operands), parts),
        out_shape=(
            pltpu.VMEM((3 * units, 2 * rows), bf16),
            pltpu.VMEM((1, 2 * rows), jnp.float32),
            share,
            share,
            share,
            share,
        ),
        in_specs=[pl.BlockSpec(memory_space=pltpu.SMEM)]
        + [pl.BlockSpec(memory_space=pltpu.VMEM)] * (len(operands) + 4),
        out_specs=[pl.BlockSpec(memory_space=pltpu.VMEM)] * 6,
        scratch_shapes=[pltpu.VMEM((2 * rows, 2 * units), bf16)],
        compiler_params=pltpu.CompilerParams(vmem_limit_bytes=VMEM),
        cost_estimate=pl.CostEstimate(flops=1, bytes_accessed=1, transcendentals=0),
        name="activations",
    )(where, *in_vmem(*tables, *operands, *weights))


def weight_grads_kernel(sources, x_places, dy_places, loaded, parts, flag_ref, *refs):
    operands, refs = list(refs[:loaded]), refs[loaded:]
    count = len(sources)
    own, other, refs = refs[:count], refs[count : 2 * count], refs[2 * count :]
    outs = refs[:3]
    held, acts, results, sems, out_sems = refs[3:]
    units, width = outs[0].shape[1:]
    rows = own[0].shape[1] // 2
    half = rows // 2
    chunk = width // parts
    copies = []
    for part in range(parts):
        columns = pl.ds(part * chunk, chunk)
        copies.append([])
        for i in range(loaded):
            copies[-1].append(
                pltpu.make_async_copy(operands[i].at[:, columns], held.at[i, :, columns], sems.at[part, i])
            )
            copies[-1][-1].start()
    for i in range(loaded):
        operands[i] = held.at[i]
    x_pieces, dy_pieces = pieces_of(x_places, operands), pieces_of(dy_places, operands)
    tiles = [(one ^ core, two ^ core) for one, two in sources for core in (0, CORE)]
    first = lax.broadcasted_iota(jnp.int32, (1, rows), 1) < half

    def tile_of(groups_of, place):
        return groups_of[place // 2][:, pl.ds(place % 2 * rows, rows)]

    for place, (one, two) in enumerate(tiles):
        from_one = [tile[0] for tile in tiles].index(one ^ ACROSS_Y)
        from_two = [tile[1] for tile in tiles].index(two ^ ACROSS_Y)
        arrived = jnp.where(first, tile_of(other, from_one), tile_of(other, from_two))
        acts[:, pl.ds(place * rows, rows)] = jnp.where(flag_ref[0] == 1, arrived, tile_of(own, place))
    sent = []
    for part in range(parts):
        for copy in copies[part]:
            copy.wait()
        columns = pl.ds(part * chunk, chunk)
        x, dy = rows_of(x_pieces, columns), rows_of(dy_pieces, columns)
        both = jnp.dot(acts[pl.ds(0, 2 * units), :], x, preferred_element_type=jnp.float32)
        results[part, pl.ds(0, 2 * units), :] = both.astype(jnp.bfloat16)
        down = jnp.dot(acts[pl.ds(2 * units, units), :], dy, preferred_element_type=jnp.float32)
        results[part, pl.ds(2 * units, units), :] = down.astype(jnp.bfloat16)
        for i, out in enumerate(outs):
            sent.append(
                pltpu.make_async_copy(
                    results.at[part, pl.ds(i * units, units), :], out.at[0, :, columns], out_sems.at[part, i]
                )
            )
            sent[-1].start()
    for copy in sent:
        copy.wait()


def weight_grads(sources, flag, groups, own, other):
    parts = 4
    operands, x_places, dy_places = [], [], []
    for held, x_of, dy_of in groups:
        x_places += [(i + len(operands), start, size) for i, start, size in x_of]
        dy_places += [(i + len(operands), start, size) for i, start, size in dy_of]
        operands += held
    rows, width = operands[0].shape
    loaded = len(operands)
    units = own[0].shape[0] // 3
    total = sum(size for _, _, size in x_places)
    bf16 = jnp.bfloat16
    rest = in_vmem(*own, *other)
    return pl.pallas_call(
        functools.partial(weight_grads_kernel, sources, x_places, dy_places, loaded, parts),
        out_shape=(jax.ShapeDtypeStruct((1, units, width), bf16),) * 3,
        in_specs=[pl.BlockSpec(memory_space=pltpu.SMEM)]
        + [pl.BlockSpec(memory_space=pl.ANY)] * loaded
        + [pl.BlockSpec(memory_space=pltpu.VMEM)] * len(rest),
        out_specs=[pl.BlockSpec(memory_space=pl.ANY)] * 3,
        scratch_shapes=[
            pltpu.VMEM((loaded, rows, width), bf16),
            pltpu.VMEM((3 * units, total), bf16),
            pltpu.VMEM((parts, 3 * units, width // parts), bf16),
            pltpu.SemaphoreType.DMA((parts, loaded)),
            pltpu.SemaphoreType.DMA((parts, 3)),
        ],
        compiler_params=pltpu.CompilerParams(vmem_limit_bytes=28 * 1024 * 1024),
        cost_estimate=pl.CostEstimate(flops=1, bytes_accessed=1, transcendentals=0),
        name="weight_grads",
    )(flag, *[pltpu.with_memory_space_constraint(value, pltpu.HBM) for value in operands], *rest)


CORE, ACROSS_X, ACROSS_Y = 1, 2, 4


def whole_shards(tokens, cotangent, gate_weight, up_weight, down_weight, expert_ids, gates, swap_flags):
    expert_count = lax.axis_size("expert")
    half_axis = expert_count // 2
    me, group = lax.axis_index("expert"), lax.axis_index("dp")
    half = tokens.shape[0] // 2
    parts = lax.axis_size("dp")
    f32, bf16 = jnp.float32, jnp.bfloat16
    own_flag = pair_lookup(jnp.reshape(me, (1,)), swap_flags, half_axis)
    where = jnp.stack([me, group]).astype(jnp.int32)
    weights = (jnp.concatenate([gate_weight[0], up_weight[0]]), down_weight[0])

    def expert_swap(value, by):
        return swap(value, "expert", by)

    rows = 2 * half
    own_block = [tokens, cotangent, expert_swap(tokens, CORE), expert_swap(cotangent, CORE)]
    own_block = (own_block, [(0, 0, rows), (2, 0, rows)], [(1, 0, rows), (3, 0, rows)])
    a, b = {}, {}
    a[0], b[0] = pack(tokens, cotangent)
    a[2], b[4] = expert_swap(a[0], ACROSS_X), expert_swap(b[0], ACROSS_Y)
    a[4], b[2] = expert_swap(a[0], ACROSS_Y), expert_swap(b[0], ACROSS_X)

    named = expert_ids[:, :, None] == jnp.arange(expert_count, dtype=jnp.int32)[None, None, :]
    table = jnp.sum(jnp.where(named, gates[:, :, None].astype(f32), 0), axis=1)
    tables = {0: jnp.concatenate([table.T, expert_swap(table.T, CORE)])}
    tables[2], tables[4] = expert_swap(tables[0], ACROSS_X), expert_swap(tables[0], ACROSS_Y)

    scores, groups = [], []
    barrier = lax.optimization_barrier

    def group_of(one, two):
        messages = [one, two, expert_swap(one, CORE), expert_swap(two, CORE)]
        return messages, [(i, 0, half) for i in range(4)], [(i, half, half) for i in range(4)]

    def work(one, two, held):
        acts, score, keep_near, keep_far, give_near, give_far = activations(
            parts, where, (tables[one], tables[two]), held, weights
        )
        scores.append(score)
        groups.append(held)
        return acts, expert_swap(give_far, CORE), (keep_near, keep_far, expert_swap(give_near, CORE))

    def to_neighbour(far, share):
        keep_near, keep_far, near = share
        return keep_near + near, swap(keep_far + far, "dp", 1)

    def to_far(near, arrived):
        near = near + arrived
        return near[0].astype(f32), swap(near[1], "dp", 2)

    acts_a, far_a, share_a = work(0, 0, own_block)
    a[2], b[4], tables[2], tables[4], acts_a, far_a = barrier((a[2], b[4], tables[2], tables[4], acts_a, far_a))
    a[6], b[6] = expert_swap(a[2], ACROSS_Y), expert_swap(b[4], ACROSS_X)
    tables[6] = expert_swap(tables[2], ACROSS_Y)
    near_a, near_in_a = to_neighbour(far_a, share_a)
    acts_b, far_b, share_b = work(2, 4, group_of(a[2], b[4]))
    a[4], b[2], tables[6], acts_b, near_in_a, far_b = barrier((a[4], b[2], tables[6], acts_b, near_in_a, far_b))
    near_b, near_in_b = to_neighbour(far_b, share_b)
    total_a, far_in_a = to_far(near_a, near_in_a)
    acts_c, far_c, share_c = work(4, 2, group_of(a[4], b[2]))
    a[6], b[6], acts_c, far_in_a, near_in_b, far_c = barrier((a[6], b[6], acts_c, far_in_a, near_in_b, far_c))
    near_c, near_in_c = to_neighbour(far_c, share_c)
    other_a, other_b = expert_swap(acts_a, half_axis), expert_swap(acts_b, half_axis)
    acts_d, far_d, share_d = work(6, 6, group_of(a[6], b[6]))
    other_c, other_d = expert_swap(acts_c, half_axis), expert_swap(acts_d, half_axis)
    total_b, far_in_b = to_far(near_b, near_in_b)
    tiles = jnp.concatenate(scores, axis=1).reshape(expert_count, 2 * half)
    second = jnp.concatenate([tiles[:2, half:], tiles[4:6, half:], tiles[2:4, half:], tiles[6:, half:]])
    score_rows = jnp.concatenate([tiles[:, :half], second], axis=1)
    score_in = swap(score_rows, "dp", 1)
    far_d, score_in, near_in_c, other_a, other_b = barrier((far_d, score_in, near_in_c, other_a, other_b))
    near_d, near_in_d = to_neighbour(far_d, share_d)
    score_rows = score_rows + score_in
    total_c, far_in_c = to_far(near_c, near_in_c)
    score_rows, near_in_d, far_in_b, far_in_c, other_c, other_d, own_flag = barrier(
        (score_rows, near_in_d, far_in_b, far_in_c, other_c, other_d, own_flag)
    )
    total_d, far_in_d = to_far(near_d, near_in_d)
    score_rows = score_rows + swap(score_rows, "dp", 2)
    score_rows = jnp.take(score_rows.astype(bf16), jnp.arange(expert_count, dtype=jnp.int32) ^ me, axis=0)
    score_rows = lax.all_to_all(score_rows, "expert", split_axis=0, concat_axis=0, tiled=True)
    own, other = (acts_a, acts_b, acts_c, acts_d), (other_a, other_b, other_c, other_d)
    grads = weight_grads(((0, 0), (2, 4), (4, 2), (6, 6)), own_flag, groups, own, other)
    far_in_d, grads = barrier((far_in_d, grads))

    total_a, total_b = total_a + far_in_a.astype(f32), total_b + far_in_b.astype(f32)
    total_c, total_d = total_c + far_in_c.astype(f32), (total_d + far_in_d.astype(f32)).astype(bf16)
    to_x = jnp.concatenate([total_b[:half], total_c[half:]]).astype(bf16)
    to_y = jnp.concatenate([total_c[:half], total_b[half:]]).astype(bf16)
    input_grad = total_a + expert_swap(to_x, ACROSS_X).astype(f32) + expert_swap(to_y, ACROSS_Y).astype(f32)
    input_grad = input_grad + expert_swap(total_d, ACROSS_X | ACROSS_Y).astype(f32)
    gate_grad = jnp.sum(jnp.where(named, score_rows.T[:, None, :].astype(f32), 0), axis=2)
    return (input_grad.astype(bf16), gate_grad.astype(bf16), *grads)


def packed_shards(tokens, cotangent, gate_weight, up_weight, down_weight, expert_ids, gates, swap_flags):
    expert_count = lax.axis_size("expert")
    half_axis = expert_count // 2
    my_slot = lax.axis_index("expert")
    row_count, model_width = tokens.shape
    routed = expert_ids.shape[1]
    capacity = row_count * routed * 5 // (4 * expert_count)
    groups = lax.axis_size("dp")
    quarter = model_width // groups
    own_flag = pair_lookup(jnp.reshape(my_slot, (1,)), swap_flags, half_axis)[0]
    flat_ids = expert_ids.reshape(-1)
    weights = (gate_weight, up_weight, down_weight)
    arrived = from_behind((gate_weight, up_weight, down_weight), "expert", half_axis)
    weights = tuple(
        (jnp.where(own_flag == 1, fresh, stay) for fresh, stay in zip(arrived, weights))
    )
    flipped = pair_lookup(flat_ids, swap_flags, half_axis)
    target = jnp.where(flipped == 1, (flat_ids + half_axis) % expert_count, flat_ids)
    copies = row_count * routed
    onehot = (target[:, None] == jnp.arange(expert_count, dtype=jnp.int32)[None, :]).astype(
        jnp.int32
    )
    earlier = jnp.cumsum(onehot, axis=0) - onehot
    position = jnp.sum(earlier * onehot, axis=1)
    buffer_index = target * capacity + position
    source = jnp.zeros((expert_count * capacity,), jnp.int32)
    source = source.at[buffer_index].set(jnp.arange(copies, dtype=jnp.int32) + 1)
    filled = source > 0
    copy_index = jnp.maximum(source - 1, 0)
    token_index = copy_index // routed
    x_buffer = jnp.where(filled[:, None], tokens[token_index], 0)
    dy_buffer = jnp.where(filled[:, None], cotangent[token_index], 0)
    gate_buffer = jnp.where(filled, gates.reshape(-1)[copy_index], 0)
    x_rows, dy_rows, gate_rows = (
        lax.all_to_all(x_buffer, "expert", split_axis=0, concat_axis=0, tiled=True),
        lax.all_to_all(dy_buffer, "expert", split_axis=0, concat_axis=0, tiled=True),
        lax.all_to_all(gate_buffer, "expert", split_axis=0, concat_axis=0, tiled=True),
    )
    w_gate = weights[0][0]
    w_up = weights[1][0]
    w_down = weights[2][0]
    contract_last = (((1,), (1,)), ((), ()))
    pre_gate = lax.dot_general(x_rows, w_gate, contract_last, preferred_element_type=jnp.float32)
    pre_up = lax.dot_general(x_rows, w_up, contract_last, preferred_element_type=jnp.float32)
    sigma = jax.nn.sigmoid(pre_gate)
    active = pre_gate * sigma
    hidden = (active * pre_up).astype(jnp.bfloat16)
    back = lax.dot_general(dy_rows, w_down, contract_last, preferred_element_type=jnp.float32)
    score_part = jnp.sum(hidden.astype(jnp.float32) * back, axis=1)
    grad_hidden = gate_rows.astype(jnp.float32)[:, None] * back
    slope = sigma * (1.0 + pre_gate * (1.0 - sigma))
    grad_gate = (grad_hidden * pre_up * slope).astype(jnp.bfloat16)
    grad_up = (grad_hidden * active).astype(jnp.bfloat16)
    input_part = jnp.dot(grad_gate, w_gate, preferred_element_type=jnp.float32)
    input_part = input_part + jnp.dot(grad_up, w_up, preferred_element_type=jnp.float32)
    scaled = gate_rows[:, None] * dy_rows
    contract_rows = (((0,), (0,)), ((), ()))
    grad_wgate = lax.dot_general(
        grad_gate, x_rows, contract_rows, preferred_element_type=jnp.float32
    )
    grad_wup = lax.dot_general(grad_up, x_rows, contract_rows, preferred_element_type=jnp.float32)
    grad_wdown = lax.dot_general(hidden, scaled, contract_rows, preferred_element_type=jnp.float32)
    scores = lax.psum(score_part, "dp")
    input_share = lax.psum_scatter(input_part, "dp", scatter_dimension=1, tiled=True).astype(
        jnp.bfloat16
    )
    back_rows, back_scores = (
        lax.all_to_all(input_share, "expert", split_axis=0, concat_axis=0, tiled=True),
        lax.all_to_all(
            scores.astype(jnp.bfloat16), "expert", split_axis=0, concat_axis=0, tiled=True
        ),
    )
    per_copy = back_rows[buffer_index].reshape(row_count, routed, quarter)
    input_grad = jnp.sum(per_copy.astype(jnp.float32), axis=1).astype(jnp.bfloat16)
    gate_grad = back_scores[buffer_index].reshape(row_count, routed)
    gradients = (
        grad_wgate.astype(jnp.bfloat16)[None],
        grad_wup.astype(jnp.bfloat16)[None],
        grad_wdown.astype(jnp.bfloat16)[None],
    )
    return (input_grad, gate_grad, gradients[0], gradients[1], gradients[2])


def chosen(tokens, cotangent, gate_weight, up_weight, down_weight, expert_ids, gates, swap_flags):
    capacity = tokens.shape[0] * expert_ids.shape[1] * 5 // (4 * lax.axis_size("expert"))
    body = whole_shards if 2 * capacity >= tokens.shape[0] else packed_shards
    return body(tokens, cotangent, gate_weight, up_weight, down_weight, expert_ids, gates, swap_flags)


def solution(mesh):
    placed = (
        P("expert", None),
        P("expert", None),
        P("expert", "dp", None),
        P("expert", "dp", None),
        P("expert", "dp", None),
        P("expert", None),
        P("expert", None),
        P(),
    )
    return jax.shard_map(
        chosen,
        mesh=mesh,
        in_specs=placed,
        out_specs=(
            P("expert", "dp"),
            P("expert", None),
            P("expert", "dp", None),
            P("expert", "dp", None),
            P("expert", "dp", None),
        ),
        check_vma=False,
    )
```
